32 devices in a mesh: docs: 8 (over z, core), protos: 4 (over y, x).
Axes of the slice: x: 2, y: 2, z: 4, core: 2. Of those that a mesh axis runs over, the one named last changes fastest.
Arguments:
- embeddings: bfloat16 [8192, 512], P('docs'), may hold values from -12.5 to 12.5
- prototypes: bfloat16 [65536, 512], P('protos'), may hold values from -4 to 4
Outputs:
- new_prototypes: bfloat16 [65536, 512], P(('protos', 'docs'))
- column_potential: float32 [65536], P('protos')
- row_potential: float32 [8192], P('docs')
The draws below stay inside these ranges and needn't reach their ends.
All inputs are finite; a program needn't handle non-finite values.
Results may differ from the reference program's by a relative error of at most 0.0035.
Values may be sent and summed in bfloat16 or wider, within the bound.
No kernel may reach another device: no remote copies, remote signals or barrier semaphores. Data moves between devices by JAX's collectives and lax.ppermute only.
A program may use at most 256 MiB of HBM per device.

```python
import math
import jax
import jax.numpy as jnp
from jax import lax

D = 512
K = 65536
SWEEPS = 2
DOCS = 8192


def proto_table(key):
    base_table = jnp.clip(jax.random.normal(key, (K, D), jnp.float32), -4.0, 4.0)
    return base_table


def draw_prototypes(key, part):
    return proto_table(jax.random.fold_in(key, 11)).astype(jnp.bfloat16)


def draw_embeddings(key, part):
    own_key = jax.random.fold_in(key, 23)
    sub_keys = jax.random.split(own_key, 1)
    drawn_rows = jnp.clip(jax.random.normal(sub_keys[0], (DOCS, D), jnp.float32), -6.0, 6.0)
    return drawn_rows.astype(jnp.bfloat16)


def setup_inputs(seed: int = 0) -> dict:
    splits = jax.random.split(jax.random.key(seed), 3)
    return {
        "embeddings": draw_embeddings(jax.random.fold_in(splits[2], 71), 0),
        "prototypes": draw_prototypes(jax.random.fold_in(splits[2], 71), 0),
    }


def logit_block(embeddings, proto_block):
    logit_gain = 4.0 / math.sqrt(embeddings.shape[1])
    return jnp.dot(embeddings, proto_block.T, preferred_element_type=jnp.float32) * logit_gain

def reference(embeddings, prototypes):
    block_size = min(K, 2048)
    block_count = K // block_size
    block_table = prototypes.reshape(block_count, block_size, D)

    def stat_step(state_pair, proto_block):
        row_peak, row_total = state_pair
        scores = logit_block(embeddings, proto_block)
        new_peak = jnp.maximum(row_peak, lax.optimization_barrier(jnp.max(scores, axis=1)))
        row_total = row_total * jnp.exp(row_peak - new_peak) + lax.optimization_barrier(jnp.sum(jnp.exp(scores - new_peak[:, None]), axis=1))
        return ((new_peak, row_total), None)
    start_peak = jnp.full((DOCS,), -jnp.inf, dtype=jnp.float32)
    start_total = jnp.zeros((DOCS,), jnp.float32)
    (row_peak, row_total), unused = lax.scan(stat_step, (start_peak, start_total), block_table)

    def numerators(proto_block):
        return jnp.exp(logit_block(embeddings, proto_block) - row_peak[:, None])
    row_scale = 1.0 / row_total
    col_scale = jnp.zeros((K,), jnp.float32)
    for sweep_index in range(SWEEPS):

        def column_step(proto_block):
            return jnp.dot(row_scale, numerators(proto_block), precision=lax.Precision.HIGHEST, preferred_element_type=jnp.float32)
        col_total = lax.map(column_step, block_table).reshape(K)
        col_scale = 1.0 / (K * col_total)

        def row_step(row_sum, block_pair):
            proto_block, col_part = block_pair
            return (row_sum + jnp.dot(numerators(proto_block), col_part, precision=lax.Precision.HIGHEST, preferred_element_type=jnp.float32), None)
        row_sum, unused = lax.scan(row_step, jnp.zeros((DOCS,), jnp.float32), (block_table, col_scale.reshape(block_count, block_size)))
        row_scale = 1.0 / (DOCS * row_sum)

    def update_step(block_pair):
        proto_block, col_part = block_pair
        assignment = (numerators(proto_block) * (DOCS * row_scale)[:, None] * col_part[None, :]).astype(jnp.bfloat16)
        partials = jnp.dot(assignment.T, embeddings, preferred_element_type=jnp.float32)
        return (partials * lax.rsqrt(lax.optimization_barrier(jnp.mean(partials * partials, axis=1, keepdims=True)) + 1e-06)).astype(jnp.bfloat16)
    new_prototypes = lax.map(update_step, (block_table, col_scale.reshape(block_count, block_size))).reshape(K, D)
    return (new_prototypes, jnp.log(DOCS * col_scale), jnp.log(row_scale * row_total))
```

```python
import functools
import math

import jax
import jax.numpy as jnp
from jax import lax
from jax.experimental import pallas as pl
from jax.experimental.pallas import tpu as pltpu
from jax.sharding import PartitionSpec as P

SWEEPS = 2
VMEM_LIMIT = 26 << 20
SUB = 512
F32 = jnp.float32
BF16 = jnp.bfloat16


def params():
    return pltpu.CompilerParams(vmem_limit_bytes=VMEM_LIMIT)


def whole():
    return pl.BlockSpec(memory_space=pltpu.VMEM)


def transposed_dot(a, b):
    return lax.dot_general(a, b, (((1,), (1,)), ((), ())), preferred_element_type=F32)


def rows_of(index, size):
    return pl.ds(pl.multiple_of(index * size, size), size)


def stats_kernel(gain, e_ref, p_ref, num_ref, peak_ref, lse_ref, s0, s1, total):
    step = pl.program_id(0)
    steps = pl.num_programs(0) - 1

    def finish(scores_ref, block):
        scores = scores_ref[...]
        peak = jnp.max(scores, axis=0, keepdims=True)
        num = jnp.exp2((scores - peak) * gain)
        num_ref[rows_of(block, SUB), :] = num.astype(BF16)
        peak_ref[pl.ds(block, 1), :] = peak * gain
        total[pl.ds(block, 1), :] = jnp.sum(num, axis=0, keepdims=True)

    @pl.when(step < steps)
    def _():
        s0[...] = transposed_dot(p_ref[:SUB, :], e_ref[...])
        finish(s1, jnp.maximum(2 * step - 1, 0))
        s1[...] = transposed_dot(p_ref[SUB:, :], e_ref[...])
        finish(s0, 2 * step)

    @pl.when(step == steps)
    def _():
        finish(s1, 2 * step - 1)
        peaks = peak_ref[...]
        top = jnp.max(peaks, axis=0, keepdims=True)
        parts = total[...] * jnp.exp2(peaks - top)
        lse_ref[...] = top + jnp.log2(jnp.sum(parts, axis=0, keepdims=True))


def stats(e, p, gain):
    docs, width = e.shape
    protos = p.shape[0]
    steps = protos // (2 * SUB)
    blocks = protos // SUB
    return pl.pallas_call(
        functools.partial(stats_kernel, gain),
        grid=(steps + 1,),
        in_specs=[
            pl.BlockSpec((docs, width), lambda i: (0, 0)),
            pl.BlockSpec((2 * SUB, width), lambda i: (jnp.minimum(i, steps - 1), 0)),
        ],
        out_specs=[whole(), whole(), whole()],
        out_shape=[
            pltpu.VMEM((protos, docs), BF16),
            jax.ShapeDtypeStruct((blocks, docs), F32),
            jax.ShapeDtypeStruct((1, docs), F32),
        ],
        scratch_shapes=[
            pltpu.VMEM((SUB, docs), F32),
            pltpu.VMEM((SUB, docs), F32),
            pltpu.VMEM((blocks, docs), F32),
        ],
        compiler_params=params(),
    )(e, p)


def split_rows(row):
    high = row.astype(BF16)
    rest = row - high.astype(F32)
    mid = rest.astype(BF16)
    low = (rest - mid.astype(F32)).astype(BF16)
    pad = jnp.zeros((5, row.shape[1]), BF16)
    return jnp.concatenate([high, mid, low, pad], axis=0)


def columns_kernel(num_ref, peak_ref, lse_ref, r_ref, out_ref):
    blocks = peak_ref.shape[0]

    def body(b, carry):
        weight = jnp.exp2(peak_ref[pl.ds(b, 1), :] - lse_ref[...]) * r_ref[...]
        part = transposed_dot(split_rows(weight), num_ref[rows_of(b, SUB), :])
        out_ref[:, rows_of(b, SUB)] = jnp.sum(part, axis=0, keepdims=True)
        return carry

    lax.fori_loop(0, blocks, body, 0, unroll=2)


def columns(num, peaks, lse, r):
    return pl.pallas_call(
        columns_kernel,
        in_specs=[whole()] * 4,
        out_specs=whole(),
        out_shape=jax.ShapeDtypeStruct((1, num.shape[0]), F32),
        compiler_params=params(),
    )(num, peaks, lse, r)


def rows_kernel(num_ref, peak_ref, lse_ref, cs_ref, out_ref):
    blocks = peak_ref.shape[0]

    def body(b, total):
        weight = jnp.exp2(peak_ref[pl.ds(b, 1), :] - lse_ref[...])
        part = jnp.dot(
            split_rows(cs_ref[:, rows_of(b, SUB)]),
            num_ref[rows_of(b, SUB), :],
            preferred_element_type=F32,
        )
        return total + weight * part

    total = lax.fori_loop(
        0, blocks, body, jnp.zeros((8, num_ref.shape[1]), F32), unroll=2
    )
    out_ref[...] = jnp.sum(total, axis=0, keepdims=True)


def row_sums(num, peaks, lse, cs):
    return pl.pallas_call(
        rows_kernel,
        in_specs=[whole()] * 4,
        out_specs=whole(),
        out_shape=jax.ShapeDtypeStruct((1, num.shape[1]), F32),
        compiler_params=params(),
    )(num, peaks, lse, cs)


UPDATE_DOCS = 512
UPDATE_SUB = 256


def update_kernel(gain, place_ref, p_ref, e_ref, v_ref, cs_ref, out_ref, scores, acc):
    del place_ref
    step = pl.program_id(0)
    own = p_ref.shape[0]
    parts = own // UPDATE_SUB

    @pl.when(step == 0)
    def _():
        acc[...] = jnp.zeros_like(acc)

    def score(k):
        scores[k % 2] = transposed_dot(
            p_ref[k * UPDATE_SUB : (k + 1) * UPDATE_SUB, :], e_ref[...]
        )

    score(0)
    for k in range(parts):
        if k + 1 < parts:
            score(k + 1)
        share = jnp.exp2(scores[k % 2] * gain + v_ref[...]).astype(BF16)
        place = slice(k * UPDATE_SUB, (k + 1) * UPDATE_SUB)
        acc[place, :] += jnp.dot(share, e_ref[...], preferred_element_type=F32)

    @pl.when(step == pl.num_programs(0) - 1)
    def _():
        summed = acc[...] * cs_ref[...]
        square = jnp.mean(summed * summed, axis=1, keepdims=True)
        out_ref[...] = (summed * lax.rsqrt(square + 1e-06)).astype(BF16)


def update(place, p, e_all, v_all, cs_own, gain):
    own = cs_own.shape[0]
    docs, width = e_all.shape
    return pl.pallas_call(
        functools.partial(update_kernel, gain),
        grid_spec=pltpu.PrefetchScalarGridSpec(
            num_scalar_prefetch=1,
            grid=(docs // UPDATE_DOCS,),
            in_specs=[
                pl.BlockSpec((own, width), lambda i, place: (place[0], 0)),
                pl.BlockSpec((UPDATE_DOCS, width), lambda i, place: (i, 0)),
                pl.BlockSpec((1, UPDATE_DOCS), lambda i, place: (0, i)),
                pl.BlockSpec((own, 1), lambda i, place: (0, 0)),
            ],
            out_specs=pl.BlockSpec((own, width), lambda i, place: (0, 0)),
            scratch_shapes=[
                pltpu.VMEM((2, UPDATE_SUB, UPDATE_DOCS), F32),
                pltpu.VMEM((own, width), F32),
            ],
        ),
        out_shape=jax.ShapeDtypeStruct((own, width), BF16),
        compiler_params=params(),
    )(place, p, e_all, v_all, cs_own)


def swap(x, axis, bit):
    size = lax.axis_size(axis)
    return lax.ppermute(x, axis, [(i, i ^ bit) for i in range(size)])


def bits(axis):
    bit = 1
    while bit < lax.axis_size(axis):
        yield bit
        bit *= 2


def reduce_over(x, axis, combine):
    for bit in bits(axis):
        x = combine(x, swap(x, axis, bit))
    return x


def gather_over(x, axis):
    for bit in bits(axis):
        other = swap(x, axis, bit)
        upper = (lax.axis_index(axis) & bit) != 0
        x = jnp.where(
            upper,
            jnp.concatenate([other, x], axis=1),
            jnp.concatenate([x, other], axis=1),
        )
    return x


def log_add(a, b):
    top = jnp.maximum(a, b)
    return top + jnp.log2(jnp.exp2(a - top) + jnp.exp2(b - top))


def on_device(embeddings, prototypes):
    docs, width = embeddings.shape
    protos = prototypes.shape[0]
    doc_ranks = lax.axis_size("docs")
    total_docs = docs * doc_ranks
    total_protos = protos * lax.axis_size("protos")
    own = protos // doc_ranks
    gain = 4.0 / math.sqrt(width) / math.log(2.0)
    place = lax.axis_index("docs")

    e_all = lax.all_gather(embeddings, "docs", tiled=True)
    num, peaks, lse = stats(embeddings, prototypes, gain)
    num = pltpu.with_memory_space_constraint(num, pltpu.VMEM)
    lse = reduce_over(lse, "protos", log_add)
    r = jnp.ones((1, docs), F32)
    for sweep_index in range(SWEEPS):
        col_total = reduce_over(columns(num, peaks, lse, r), "docs", jnp.add)
        cs = 1.0 / (total_protos * col_total)
        row_sum = reduce_over(row_sums(num, peaks, lse, cs), "protos", jnp.add)
        r = 1.0 / (total_docs * row_sum)
    column_potential = jnp.log(total_docs * cs)
    row_potential = jnp.log(r)
    v_all = gather_over(jnp.log2(r * total_docs) - lse, "docs")
    cs_own = lax.dynamic_slice(cs, (0, place * own), (1, own)).reshape(own, 1)
    new_prototypes = update(
        place.reshape(1).astype(jnp.int32),
        pltpu.with_memory_space_constraint(prototypes, pltpu.HBM),
        pltpu.with_memory_space_constraint(e_all, pltpu.HBM),
        v_all,
        cs_own,
        gain,
    )
    return (new_prototypes, column_potential.reshape(-1), row_potential.reshape(-1))


def solution(mesh):
    placed = (P("docs", None), P("protos", None))
    return jax.shard_map(
        on_device,
        mesh=mesh,
        in_specs=placed,
        out_specs=(P(("protos", "docs"), None), P("protos"), P("docs")),
        check_vma=False,
    )
```

```python
import functools
import math

import jax
import jax.numpy as jnp
from jax import lax
from jax.experimental import pallas as pl
from jax.experimental.pallas import tpu as pltpu
from jax.sharding import PartitionSpec as P

SWEEPS = 2
VMEM_LIMIT = 26 << 20
BLOCK = 1024
FIRST = 256
DOC_TILE = 256
LARGE = 2.0**60
CHUNK = 128
COLUMN_GROUP = 32
ROW_GROUP = 16
ROW_TAKEN = 10
F32 = jnp.float32
BF16 = jnp.bfloat16


def params():
    return pltpu.CompilerParams(vmem_limit_bytes=VMEM_LIMIT)


def whole():
    return pl.BlockSpec(memory_space=pltpu.VMEM)


def in_vmem(x):
    return pltpu.with_memory_space_constraint(x, pltpu.VMEM)


def in_hbm(x):
    return pltpu.with_memory_space_constraint(x, pltpu.HBM)


def transposed_dot(a, b):
    return lax.dot_general(a, b, (((1,), (1,)), ((), ())), preferred_element_type=F32)


def rows_of(index, size):
    return pl.ds(pl.multiple_of(index * size, size), size)


def stats_kernel(gain, e_ref, p_ref, p_any, num_ref, shift_ref, lse_ref, total, p_buf):
    step = pl.program_id(0)
    docs = e_ref.shape[0]
    tiles = [slice(d, d + DOC_TILE) for d in range(0, docs, DOC_TILE)]

    @pl.when(step == 0)
    def _():
        first = transposed_dot(p_ref[:FIRST, :], e_ref[...])
        shift_ref[...] = jnp.max(first, axis=0, keepdims=True)

    def fill(block_ref, block):
        sums = []
        for tile in tiles:
            scores = transposed_dot(block_ref[...], e_ref[tile, :])
            num = jnp.exp2((scores - shift_ref[:, tile]) * gain)
            num_ref[rows_of(block, BLOCK), tile] = num.astype(BF16)
            sums.append(jnp.sum(num, axis=0, keepdims=True))
        total[pl.ds(block, 1), :] = jnp.concatenate(sums, axis=1)

    fill(p_ref, step)

    @pl.when(step == pl.num_programs(0) - 1)
    def _():
        found = jnp.sum(total[...], axis=0, keepdims=True)
        fits = jnp.min(jnp.where(found < LARGE, 1.0, 0.0))

        @pl.when(fits < 0.5)
        def _():
            def peak(block, carry):
                pltpu.sync_copy(p_any.at[rows_of(block, BLOCK)], p_buf)
                for tile in tiles:
                    scores = transposed_dot(p_buf[...], e_ref[tile, :])
                    top = jnp.max(scores, axis=0, keepdims=True)
                    shift_ref[:, tile] = jnp.maximum(shift_ref[:, tile], top)
                return carry

            def again(block, carry):
                pltpu.sync_copy(p_any.at[rows_of(block, BLOCK)], p_buf)
                fill(p_buf, block)
                return carry

            blocks = total.shape[0]
            lax.fori_loop(0, blocks, peak, 0)
            lax.fori_loop(0, blocks, again, 0)

        found = jnp.sum(total[...], axis=0, keepdims=True)
        shift = shift_ref[...] * gain
        shift_ref[...] = shift
        lse_ref[...] = shift + jnp.log2(found)


def stats(e, p, gain):
    docs, width = e.shape
    protos = p.shape[0]
    blocks = protos // BLOCK
    return pl.pallas_call(
        functools.partial(stats_kernel, gain),
        grid=(blocks,),
        in_specs=[
            pl.BlockSpec((docs, width), lambda i: (0, 0)),
            pl.BlockSpec((BLOCK, width), lambda i: (i, 0)),
            pl.BlockSpec(memory_space=pl.ANY),
        ],
        out_specs=[whole(), whole(), whole()],
        out_shape=[
            pltpu.VMEM((protos, docs), BF16),
            pltpu.VMEM((1, docs), F32),
            pltpu.VMEM((1, docs), F32),
        ],
        scratch_shapes=[
            pltpu.VMEM((blocks, docs), F32),
            pltpu.VMEM((BLOCK, width), BF16),
        ],
        compiler_params=params(),
    )(e, p, p)


def split(x):
    high = x.astype(BF16)
    rest = x - high.astype(F32)
    mid = rest.astype(BF16)
    low = (rest - mid.astype(F32)).astype(BF16)
    return [part.astype(F32) for part in (high, mid, low)]


def columns_kernel(num_ref, w_ref, out_ref, turned):
    docs = num_ref.shape[1]
    taken = turned.shape[0]
    w = w_ref[...]
    rows = split(w[:, :taken]) + [jnp.zeros((CHUNK - 3, taken), F32)]
    turned[...] = jnp.concatenate(rows, axis=0).T.astype(BF16)
    lane = lax.broadcasted_iota(jnp.int32, out_ref.shape, 1)

    def body(group, found):
        base = pl.multiple_of(group * COLUMN_GROUP * CHUNK, CHUNK)
        part = jnp.dot(
            num_ref[pl.ds(base, COLUMN_GROUP * CHUNK), :taken],
            turned[...],
            preferred_element_type=F32,
        )
        for k in range(COLUMN_GROUP):
            here = part[k * CHUNK : (k + 1) * CHUNK]
            place = pl.ds(pl.multiple_of(base + k * CHUNK, CHUNK), CHUNK)
            for d in range(taken, docs, CHUNK):
                here += num_ref[place, d : d + CHUNK].astype(F32) * w[:, d : d + CHUNK]
            column = jnp.sum(here, axis=1, keepdims=True)
            found = jnp.where(lane == group * COLUMN_GROUP + k, column, found)
        return found

    groups = num_ref.shape[0] // (COLUMN_GROUP * CHUNK)
    out_ref[...] = lax.fori_loop(0, groups, body, jnp.ones(out_ref.shape, F32))


def chunk_lanes(protos):
    return -(-protos // (CHUNK * CHUNK)) * CHUNK


def columns(num, w):
    protos, docs = num.shape
    return pl.pallas_call(
        columns_kernel,
        in_specs=[whole()] * 2,
        out_specs=whole(),
        out_shape=pltpu.VMEM((CHUNK, chunk_lanes(protos)), F32),
        scratch_shapes=[pltpu.VMEM((docs // 2, CHUNK), BF16)],
        compiler_params=params(),
    )(num, in_vmem(w))


def rows_kernel(num_ref, w_ref, cs_ref, out_ref, parts):
    docs = num_ref.shape[1]
    turned = cs_ref[...]
    for j, part in enumerate(split(turned.T)):
        parts[j] = part
    lane = lax.broadcasted_iota(jnp.int32, turned.shape, 1)

    def body(group, carry):
        added, product = carry
        base = pl.multiple_of(group * ROW_GROUP * CHUNK, CHUNK)
        rows = [
            jnp.concatenate(
                [parts[j, pl.ds(group * ROW_GROUP + k, 1), :] for k in range(ROW_TAKEN)], axis=1
            )
            for j in range(3)
        ]
        rows.append(jnp.zeros((5, ROW_TAKEN * CHUNK), F32))
        product = product + jnp.dot(
            jnp.concatenate(rows, axis=0).astype(BF16),
            num_ref[pl.ds(base, ROW_TAKEN * CHUNK), :],
            preferred_element_type=F32,
        )
        for k in range(ROW_TAKEN, ROW_GROUP):
            here = jnp.where(lane == group * ROW_GROUP + k, turned, 0.0)
            column = jnp.sum(here, axis=1, keepdims=True)
            place = pl.ds(pl.multiple_of(base + k * CHUNK, CHUNK), CHUNK)
            scaled = num_ref[place, :].astype(F32) * column
            added = added + jnp.sum(scaled.reshape(CHUNK // 8, 8, docs), axis=0)
        return added, product

    groups = num_ref.shape[0] // (ROW_GROUP * CHUNK)
    zero = jnp.zeros((8, docs), F32)
    added, product = lax.fori_loop(0, groups, body, (zero, zero))
    out_ref[...] = w_ref[...] * jnp.sum(added + product, axis=0, keepdims=True)


def row_sums(num, w, cs):
    docs = num.shape[1]
    return pl.pallas_call(
        rows_kernel,
        in_specs=[whole()] * 3,
        out_specs=whole(),
        out_shape=pltpu.VMEM((1, docs), F32),
        scratch_shapes=[pltpu.VMEM((3, cs.shape[1], CHUNK), F32)],
        compiler_params=params(),
    )(num, in_vmem(w), in_vmem(cs))


UPDATE_DOCS = 512
UPDATE_SUB = 256


def update_kernel(gain, place_ref, p_ref, e_ref, v_ref, cs_ref, out_ref, scores, acc):
    step = pl.program_id(0)
    own = p_ref.shape[0]
    parts = own // UPDATE_SUB

    @pl.when(step == 0)
    def _():
        acc[...] = jnp.zeros_like(acc)

    def score(k):
        scores[k % 2] = transposed_dot(
            p_ref[k * UPDATE_SUB : (k + 1) * UPDATE_SUB, :], e_ref[...]
        )

    score(0)
    for k in range(parts):
        if k + 1 < parts:
            score(k + 1)
        share = jnp.exp2(scores[k % 2] * gain + v_ref[...]).astype(BF16)
        place = slice(k * UPDATE_SUB, (k + 1) * UPDATE_SUB)
        acc[place, :] += jnp.dot(share, e_ref[...], preferred_element_type=F32)

    @pl.when(step == pl.num_programs(0) - 1)
    def _():
        lane = lax.broadcasted_iota(jnp.int32, cs_ref.shape, 1)
        chunks = own // CHUNK
        for k in range(chunks):
            here = jnp.where(lane == place_ref[0] * chunks + k, cs_ref[...], 0.0)
            place = slice(k * CHUNK, (k + 1) * CHUNK)
            summed = acc[place, :] * jnp.sum(here, axis=1, keepdims=True)
            square = jnp.mean(summed * summed, axis=1, keepdims=True)
            out_ref[place, :] = (summed * lax.rsqrt(square + 1e-06)).astype(BF16)


def update(place, p, e_all, v_all, cs, own, gain):
    docs, width = e_all.shape
    return pl.pallas_call(
        functools.partial(update_kernel, gain),
        grid_spec=pltpu.PrefetchScalarGridSpec(
            num_scalar_prefetch=1,
            grid=(docs // UPDATE_DOCS,),
            in_specs=[
                pl.BlockSpec((own, width), lambda i, place: (place[0], 0)),
                pl.BlockSpec((UPDATE_DOCS, width), lambda i, place: (i, 0)),
                pl.BlockSpec((1, UPDATE_DOCS), lambda i, place: (0, i)),
                pl.BlockSpec(cs.shape, lambda i, place: (0, 0)),
            ],
            out_specs=pl.BlockSpec((own, width), lambda i, place: (0, 0)),
            scratch_shapes=[
                pltpu.VMEM((2, UPDATE_SUB, UPDATE_DOCS), F32),
                pltpu.VMEM((own, width), F32),
            ],
        ),
        out_shape=jax.ShapeDtypeStruct((own, width), BF16),
        compiler_params=params(),
    )(place, in_hbm(p), in_hbm(e_all), v_all, cs)


def swap(x, axis, bit):
    size = lax.axis_size(axis)
    return lax.ppermute(x, axis, [(i, i ^ bit) for i in range(size)])


def bits(axis):
    bit = 1
    while bit < lax.axis_size(axis):
        yield bit
        bit *= 2


def reduce_over(x, axis, combine):
    for bit in bits(axis):
        x = combine(x, swap(x, axis, bit))
    return x


def gather_over(x, axis):
    for bit in bits(axis):
        other = swap(x, axis, bit)
        upper = (lax.axis_index(axis) & bit) != 0
        x = jnp.where(
            upper,
            jnp.concatenate([other, x], axis=1),
            jnp.concatenate([x, other], axis=1),
        )
    return x


def log_add(a, b):
    top = jnp.maximum(a, b)
    return top + jnp.log2(jnp.exp2(a - top) + jnp.exp2(b - top))


def on_device(embeddings, prototypes):
    docs, width = embeddings.shape
    protos = prototypes.shape[0]
    doc_ranks = lax.axis_size("docs")
    total_docs = docs * doc_ranks
    total_protos = protos * lax.axis_size("protos")
    own = protos // doc_ranks
    gain = 4.0 / math.sqrt(width) / math.log(2.0)

    e_all = lax.all_gather(embeddings, "docs", tiled=True)
    num, shift, lse = stats(embeddings, in_hbm(prototypes), gain)
    num = in_vmem(num)
    lse = reduce_over(lse, "protos", log_add)
    w = jnp.exp2(shift - lse)
    weight = w
    for sweep_index in range(SWEEPS):
        col_total = reduce_over(columns(num, weight), "docs", jnp.add)
        cs = 1.0 / (total_protos * col_total)
        row_sum = reduce_over(row_sums(num, w, cs), "protos", jnp.add)
        r = 1.0 / (total_docs * row_sum)
        weight = w * r
    v_all = gather_over(jnp.log2(r * total_docs) - lse, "docs")
    place = lax.axis_index("docs").reshape(1).astype(jnp.int32)
    new_prototypes = update(place, prototypes, e_all, v_all, cs, own, gain)
    column_potential = jnp.log(total_docs * cs.T.reshape(-1)[:protos])
    row_potential = jnp.log(r).reshape(-1)
    return (new_prototypes, column_potential, row_potential)


def solution(mesh):
    placed = (P("docs", None), P("protos", None))
    return jax.shard_map(
        on_device,
        mesh=mesh,
        in_specs=placed,
        out_specs=(P(("protos", "docs"), None), P("protos"), P("docs")),
        check_vma=False,
    )
```

```python
import functools
import math

import jax
import jax.numpy as jnp
from jax import lax
from jax.experimental import pallas as pl
from jax.experimental.pallas import tpu as pltpu
from jax.sharding import PartitionSpec as P

SWEEPS = 2
VMEM_LIMIT = 26 << 20
BLOCK = 1024
FIRST = 256
DOC_TILE = 256
LARGE = 2.0**60
CHUNK = 128
COLUMN_GROUP = 32
ROW_GROUP = 16
ROW_TAKEN = 10
OWN_FIRST = 128
UPDATE_ROWS = 256
F32 = jnp.float32
BF16 = jnp.bfloat16


def params():
    return pltpu.CompilerParams(vmem_limit_bytes=VMEM_LIMIT)


def whole():
    return pl.BlockSpec(memory_space=pltpu.VMEM)


def in_vmem(x):
    return pltpu.with_memory_space_constraint(x, pltpu.VMEM)


def in_hbm(x):
    return pltpu.with_memory_space_constraint(x, pltpu.HBM)


def transposed_dot(a, b):
    return lax.dot_general(a, b, (((1,), (1,)), ((), ())), preferred_element_type=F32)


def rows_of(index, size):
    return pl.ds(pl.multiple_of(index * size, size), size)


def stats_kernel(gain, place_ref, e_ref, p_ref, p_any, num_ref, shift_ref, lse_ref, own_ref, total, p_buf):
    step = pl.program_id(0)
    docs = e_ref.shape[0]
    tiles = [slice(d, d + DOC_TILE) for d in range(0, docs, DOC_TILE)]

    @pl.when(step == 0)
    def _():
        first = transposed_dot(p_ref[:FIRST, :], e_ref[...])
        shift_ref[...] = jnp.max(first, axis=0, keepdims=True)

    def fill(block_ref, block):
        sums = []
        for tile in tiles:
            scores = transposed_dot(block_ref[...], e_ref[tile, :])
            num = jnp.exp2((scores - shift_ref[:, tile]) * gain)
            num_ref[rows_of(block, BLOCK), tile] = num.astype(BF16)
            sums.append(jnp.sum(num, axis=0, keepdims=True))
        total[pl.ds(block, 1), :] = jnp.concatenate(sums, axis=1)

    fill(p_ref, step)
    own = own_ref.shape[0]
    count, per = max(own // BLOCK, 1), max(BLOCK // own, 1)
    for j in range(count):

        @pl.when(step == place_ref[0] * count // per + j)
        def _():
            offset = pl.multiple_of((place_ref[0] % per) * own, 16) if per > 1 else 0
            size = min(own, BLOCK)
            own_ref[j * size : (j + 1) * size, :] = p_ref[pl.ds(offset, size), :]

    @pl.when(step == pl.num_programs(0) - 1)
    def _():
        found = jnp.sum(total[...], axis=0, keepdims=True)
        fits = jnp.min(jnp.where(found < LARGE, 1.0, 0.0))

        @pl.when(fits < 0.5)
        def _():
            def peak(block, carry):
                pltpu.sync_copy(p_any.at[rows_of(block, BLOCK)], p_buf)
                for tile in tiles:
                    scores = transposed_dot(p_buf[...], e_ref[tile, :])
                    top = jnp.max(scores, axis=0, keepdims=True)
                    shift_ref[:, tile] = jnp.maximum(shift_ref[:, tile], top)
                return carry

            def again(block, carry):
                pltpu.sync_copy(p_any.at[rows_of(block, BLOCK)], p_buf)
                fill(p_buf, block)
                return carry

            blocks = total.shape[0]
            lax.fori_loop(0, blocks, peak, 0)
            lax.fori_loop(0, blocks, again, 0)

        found = jnp.sum(total[...], axis=0, keepdims=True)
        shift = shift_ref[...] * gain
        shift_ref[...] = shift
        lse_ref[...] = shift + jnp.log2(found)


def stats(place, own, e, p, gain):
    docs, width = e.shape
    protos = p.shape[0]
    blocks = protos // BLOCK
    return pl.pallas_call(
        functools.partial(stats_kernel, gain),
        grid_spec=pltpu.PrefetchScalarGridSpec(
            num_scalar_prefetch=1,
            grid=(blocks,),
            in_specs=[
                pl.BlockSpec((docs, width), lambda i, place: (0, 0)),
                pl.BlockSpec((BLOCK, width), lambda i, place: (i, 0)),
                pl.BlockSpec(memory_space=pl.ANY),
            ],
            out_specs=[whole()] * 4,
            scratch_shapes=[
                pltpu.VMEM((blocks, docs), F32),
                pltpu.VMEM((BLOCK, width), BF16),
            ],
        ),
        out_shape=[
            pltpu.VMEM((protos, docs), BF16),
            pltpu.VMEM((1, docs), F32),
            pltpu.VMEM((1, docs), F32),
            pltpu.VMEM((own, width), BF16),
        ],
        compiler_params=params(),
    )(place, e, p, p)


def split(x):
    high = x.astype(BF16)
    rest = x - high.astype(F32)
    mid = rest.astype(BF16)
    low = (rest - mid.astype(F32)).astype(BF16)
    return [part.astype(F32) for part in (high, mid, low)]


def columns_kernel(num_ref, w_ref, num_out, out_ref, turned):
    del num_out
    docs = num_ref.shape[1]
    taken = turned.shape[0]
    w = w_ref[...]
    rows = split(w[:, :taken]) + [jnp.zeros((CHUNK - 3, taken), F32)]
    turned[...] = jnp.concatenate(rows, axis=0).T.astype(BF16)
    lane = lax.broadcasted_iota(jnp.int32, out_ref.shape, 1)

    def body(group, found):
        base = pl.multiple_of(group * COLUMN_GROUP * CHUNK, CHUNK)
        part = jnp.dot(
            num_ref[pl.ds(base, COLUMN_GROUP * CHUNK), :taken],
            turned[...],
            preferred_element_type=F32,
        )
        for k in range(COLUMN_GROUP):
            here = part[k * CHUNK : (k + 1) * CHUNK]
            place = pl.ds(pl.multiple_of(base + k * CHUNK, CHUNK), CHUNK)
            for d in range(taken, docs, CHUNK):
                here += num_ref[place, d : d + CHUNK].astype(F32) * w[:, d : d + CHUNK]
            column = jnp.sum(here, axis=1, keepdims=True)
            found = jnp.where(lane == group * COLUMN_GROUP + k, column, found)
        return found

    groups = num_ref.shape[0] // (COLUMN_GROUP * CHUNK)
    out_ref[...] = lax.fori_loop(0, groups, body, jnp.ones(out_ref.shape, F32))


def chunk_lanes(protos):
    return -(-protos // (CHUNK * CHUNK)) * CHUNK


def columns(num, w):
    protos, docs = num.shape
    return pl.pallas_call(
        columns_kernel,
        in_specs=[whole()] * 2,
        out_specs=[whole()] * 2,
        out_shape=[pltpu.VMEM(num.shape, BF16), pltpu.VMEM((CHUNK, chunk_lanes(protos)), F32)],
        input_output_aliases={0: 0},
        scratch_shapes=[pltpu.VMEM((docs // 2, CHUNK), BF16)],
        compiler_params=params(),
    )(num, in_vmem(w))


def rows_kernel(num_ref, w_ref, cs_ref, num_out, out_ref, parts):
    del num_out
    docs = num_ref.shape[1]
    turned = cs_ref[...]
    for j, part in enumerate(split(turned.T)):
        parts[j] = part
    lane = lax.broadcasted_iota(jnp.int32, turned.shape, 1)

    def body(group, carry):
        added, product = carry
        base = pl.multiple_of(group * ROW_GROUP * CHUNK, CHUNK)
        rows = [
            jnp.concatenate(
                [parts[j, pl.ds(group * ROW_GROUP + k, 1), :] for k in range(ROW_TAKEN)], axis=1
            )
            for j in range(3)
        ]
        rows.append(jnp.zeros((5, ROW_TAKEN * CHUNK), F32))
        product = product + jnp.dot(
            jnp.concatenate(rows, axis=0).astype(BF16),
            num_ref[pl.ds(base, ROW_TAKEN * CHUNK), :],
            preferred_element_type=F32,
        )
        for k in range(ROW_TAKEN, ROW_GROUP):
            here = jnp.where(lane == group * ROW_GROUP + k, turned, 0.0)
            column = jnp.sum(here, axis=1, keepdims=True)
            place = pl.ds(pl.multiple_of(base + k * CHUNK, CHUNK), CHUNK)
            scaled = num_ref[place, :].astype(F32) * column
            added = added + jnp.sum(scaled.reshape(CHUNK // 8, 8, docs), axis=0)
        return added, product

    groups = num_ref.shape[0] // (ROW_GROUP * CHUNK)
    zero = jnp.zeros((8, docs), F32)
    added, product = lax.fori_loop(0, groups, body, (zero, zero))
    out_ref[...] = w_ref[...] * jnp.sum(added + product, axis=0, keepdims=True)


def row_sums(num, w, cs):
    docs = num.shape[1]
    return pl.pallas_call(
        rows_kernel,
        in_specs=[whole()] * 3,
        out_specs=[whole()] * 2,
        out_shape=[pltpu.VMEM(num.shape, BF16), pltpu.VMEM((1, docs), F32)],
        input_output_aliases={0: 0},
        scratch_shapes=[pltpu.VMEM((3, cs.shape[1], CHUNK), F32)],
        compiler_params=params(),
    )(num, in_vmem(w), in_vmem(cs))


def share_kernel(gain, rank_ref, e_ref, p_ref, x_ref, held_ref, num_ref, shift_ref, x_out, held_out):
    del rank_ref, held_ref, held_out

    @pl.when(pl.program_id(0) == 0)
    def _():
        x_out[...] = x_ref[...]

    own = p_ref.shape[0]
    first = transposed_dot(p_ref[:OWN_FIRST, :], e_ref[...])
    shift = jnp.max(first, axis=0, keepdims=True)
    num = jnp.exp2((transposed_dot(p_ref[...], e_ref[...]) - shift) * gain)
    num_ref[...] = num.astype(BF16)
    shift_ref[...] = shift * gain
    found = jnp.sum(num, axis=0, keepdims=True)
    fits = jnp.min(jnp.where(found < LARGE, 1.0, 0.0))

    @pl.when(fits < 0.5)
    def _():
        scores = transposed_dot(p_ref[...], e_ref[...])
        peak = jnp.max(scores, axis=0, keepdims=True)
        num_ref[...] = jnp.exp2((scores - peak) * gain).astype(BF16)
        shift_ref[...] = peak * gain


def share(rank, docs, e, p_own, x, held, gain):
    own, width = p_own.shape
    tiles = docs // DOC_TILE
    return pl.pallas_call(
        functools.partial(share_kernel, gain),
        grid_spec=pltpu.PrefetchScalarGridSpec(
            num_scalar_prefetch=1,
            grid=(tiles,),
            in_specs=[
                pl.BlockSpec((DOC_TILE, width), lambda i, rank: (rank[0] * tiles + i, 0)),
                whole(),
                whole(),
                whole(),
            ],
            out_specs=[
                pl.BlockSpec((own, DOC_TILE), lambda i, rank: (0, i)),
                pl.BlockSpec((1, DOC_TILE), lambda i, rank: (0, i)),
                whole(),
                whole(),
            ],
        ),
        out_shape=[
            pltpu.HBM((own, docs), BF16),
            pltpu.VMEM((1, docs), F32),
            pltpu.VMEM(x.shape, F32),
            pltpu.VMEM(held.shape, held.dtype),
        ],
        input_output_aliases={4: 3},
        compiler_params=params(),
    )(rank, e, in_vmem(p_own), in_vmem(x), in_vmem(held))


def update_kernel(ranks, place_ref, e_ref, v_ref, cs_ref, *refs):
    nums, shifts, out_ref = refs[:ranks], refs[ranks : 2 * ranks], refs[2 * ranks]
    rows, docs = nums[0].shape
    summed = jnp.zeros(out_ref.shape, F32)
    for k in range(ranks):
        weight = jnp.exp2(shifts[k][...] + v_ref[:, k * docs : (k + 1) * docs])
        scaled = (nums[k][...].astype(F32) * weight).astype(BF16)
        held = e_ref[rows_of(jnp.bitwise_xor(place_ref[0], k), docs), :]
        summed += jnp.dot(scaled, held, preferred_element_type=F32)
    lane = lax.broadcasted_iota(jnp.int32, cs_ref.shape, 1)
    chunks = rows // CHUNK
    first = (place_ref[0] * pl.num_programs(0) + pl.program_id(0)) * chunks
    for k in range(chunks):
        here = jnp.where(lane == first + k, cs_ref[...], 0.0)
        part = summed[k * CHUNK : (k + 1) * CHUNK] * jnp.sum(here, axis=1, keepdims=True)
        square = jnp.mean(part * part, axis=1, keepdims=True)
        out_ref[k * CHUNK : (k + 1) * CHUNK, :] = (part * lax.rsqrt(square + 1e-06)).astype(BF16)


def update(place, e_all, v, cs, nums, shifts):
    ranks = len(nums)
    own, docs = nums[0].shape
    width = e_all.shape[1]
    rows = min(UPDATE_ROWS, own)
    return pl.pallas_call(
        functools.partial(update_kernel, ranks),
        grid_spec=pltpu.PrefetchScalarGridSpec(
            num_scalar_prefetch=1,
            grid=(own // rows,),
            in_specs=[whole()] * 3
            + [pl.BlockSpec((rows, docs), lambda i, place: (i, 0))] * ranks
            + [whole()] * ranks,
            out_specs=pl.BlockSpec((rows, width), lambda i, place: (i, 0)),
        ),
        out_shape=jax.ShapeDtypeStruct((own, width), BF16),
        compiler_params=params(),
    )(place, in_vmem(e_all), in_vmem(v), in_vmem(cs), *[in_hbm(num) for num in nums], *shifts)


def swap(x, axis, bit):
    size = lax.axis_size(axis)
    return lax.ppermute(x, axis, [(i, i ^ bit) for i in range(size)])


def bits(axis):
    bit = 1
    while bit < lax.axis_size(axis):
        yield bit
        bit *= 2


def reduce_over(x, axis, combine, jobs={}):
    for bit in bits(axis):
        other = swap(x, axis, bit)
        for job in jobs.get(bit, ()):
            x = job(x)
        x = combine(x, other)
    return x


def gather_over(x, axis, jobs={}):
    for bit in bits(axis):
        other = swap(x, axis, bit)
        for job in jobs.get(bit, ()):
            x = job(x)
        x = jnp.concatenate([x, other], axis=1)
    return x


def log_add(a, b):
    top = jnp.maximum(a, b)
    return top + jnp.log2(jnp.exp2(a - top) + jnp.exp2(b - top))


def on_device(embeddings, prototypes):
    docs, width = embeddings.shape
    protos = prototypes.shape[0]
    doc_ranks = lax.axis_size("docs")
    total_docs = docs * doc_ranks
    total_protos = protos * lax.axis_size("protos")
    own = protos // doc_ranks
    gain = 4.0 / math.sqrt(width) / math.log(2.0)

    place = lax.axis_index("docs").astype(jnp.int32)

    e_all = lax.all_gather(embeddings, "docs", tiled=True)
    partner = swap(embeddings, "docs", 1)
    state = [None, None]
    nums, shifts = [None] * doc_ranks, [None] * doc_ranks

    def job_of(k, kept=True):
        def job(x):
            source, rank = (embeddings, partner, e_all)[min(k, 2)], place ^ k if k > 1 else 0 * place
            source = in_hbm(source) if k != 1 else source
            held = state[0] if kept else jnp.zeros((8, CHUNK), F32)
            nums[k], shifts[k], x, held = share(
                rank.reshape(1), docs, source, state[1], x, held, gain
            )
            if kept:
                state[0] = held
            return x

        return job

    doc_bits, proto_bits = list(bits("docs")), list(bits("protos"))
    early = {bit: [] for bit in doc_bits}
    column_jobs = {doc_bits[-1]: []}
    row_jobs = {bit: [] for bit in proto_bits}
    gather_jobs = {bit: [] for bit in doc_bits}
    for k in range(2):
        early[doc_bits[1 + k % (len(doc_bits) - 1)]].append(job_of(k))
    late = list(row_jobs.values())
    late += [gather_jobs[bit] for bit in doc_bits[1:]]
    rest = list(range(2, doc_ranks))
    for i, slot in enumerate(late):
        slot.extend(job_of(k, False) for k in rest[i :: len(late)])

    num, shift, lse, own_table = stats(
        place.reshape(1), own, in_hbm(embeddings), in_hbm(prototypes), gain
    )
    state[1] = own_table
    state[0] = num
    lse = reduce_over(lse, "protos", log_add)
    w = jnp.exp2(shift - lse)
    weight = w
    for sweep_index in range(SWEEPS):
        last = sweep_index == SWEEPS - 1
        beside = column_jobs if last else (early if sweep_index == 0 else {})
        state[0], col_local = columns(in_vmem(state[0]), weight)
        col_total = reduce_over(col_local, "docs", jnp.add, beside)
        cs = 1.0 / (total_protos * col_total)
        state[0], row_local = row_sums(in_vmem(state[0]), w, cs)
        row_sum = reduce_over(row_local, "protos", jnp.add, row_jobs if last else {})
        r = 1.0 / (total_docs * row_sum)
        weight = w * r
    v = gather_over(jnp.log2(r * total_docs) - lse, "docs", gather_jobs)
    new_prototypes = update(place.reshape(1), e_all, v, cs, nums, shifts)
    column_potential = jnp.log(total_docs * cs.T.reshape(-1)[:protos])
    row_potential = jnp.log(r).reshape(-1)
    return (new_prototypes, column_potential, row_potential)


def solution(mesh):
    placed = (P("docs", None), P("protos", None))
    return jax.shard_map(
        on_device,
        mesh=mesh,
        in_specs=placed,
        out_specs=(P(("protos", "docs"), None), P("protos"), P("docs")),
        check_vma=False,
    )
```

```python
import functools
import math

import jax
import jax.numpy as jnp
from jax import lax
from jax.experimental import pallas as pl
from jax.experimental.pallas import tpu as pltpu
from jax.sharding import PartitionSpec as P

SWEEPS = 2
VMEM_LIMIT = 26 << 20
BLOCK = 1024
FIRST = 256
DOC_TILE = 256
LARGE = 2.0**60
CHUNK = 128
COLUMN_GROUP = 32
ROW_GROUP = 16
ROW_TAKEN = 10
OWN_FIRST = 128
UPDATE_ROWS = 512
HELD = 2
F32 = jnp.float32
BF16 = jnp.bfloat16


def params():
    return pltpu.CompilerParams(vmem_limit_bytes=VMEM_LIMIT)


def whole():
    return pl.BlockSpec(memory_space=pltpu.VMEM)


def in_vmem(x):
    return pltpu.with_memory_space_constraint(x, pltpu.VMEM)


def in_hbm(x):
    return pltpu.with_memory_space_constraint(x, pltpu.HBM)


def transposed_dot(a, b):
    return lax.dot_general(a, b, (((1,), (1,)), ((), ())), preferred_element_type=F32)


def rows_of(index, size):
    return pl.ds(pl.multiple_of(index * size, size), size)


def stats_kernel(gain, place_ref, e_ref, p_ref, p_any, num_ref, shift_ref, lse_ref, own_ref, total, p_buf):
    step = pl.program_id(0)
    docs = e_ref.shape[0]
    tiles = [slice(d, d + DOC_TILE) for d in range(0, docs, DOC_TILE)]

    @pl.when(step == 0)
    def _():
        first = transposed_dot(p_ref[:FIRST, :], e_ref[...])
        shift_ref[...] = jnp.max(first, axis=0, keepdims=True)

    def fill(block_ref, block):
        sums = []
        for tile in tiles:
            scores = transposed_dot(block_ref[...], e_ref[tile, :])
            num = jnp.exp2((scores - shift_ref[:, tile]) * gain)
            num_ref[rows_of(block, BLOCK), tile] = num.astype(BF16)
            sums.append(jnp.sum(num, axis=0, keepdims=True))
        total[pl.ds(block, 1), :] = jnp.concatenate(sums, axis=1)

    fill(p_ref, step)
    own = own_ref.shape[0]
    count, per = max(own // BLOCK, 1), max(BLOCK // own, 1)
    for j in range(count):

        @pl.when(step == place_ref[0] * count // per + j)
        def _():
            offset = pl.multiple_of((place_ref[0] % per) * own, 16) if per > 1 else 0
            size = min(own, BLOCK)
            own_ref[j * size : (j + 1) * size, :] = p_ref[pl.ds(offset, size), :]

    @pl.when(step == pl.num_programs(0) - 1)
    def _():
        found = jnp.sum(total[...], axis=0, keepdims=True)
        fits = jnp.min(jnp.where(found < LARGE, 1.0, 0.0))

        @pl.when(fits < 0.5)
        def _():
            def peak(block, carry):
                pltpu.sync_copy(p_any.at[rows_of(block, BLOCK)], p_buf)
                for tile in tiles:
                    scores = transposed_dot(p_buf[...], e_ref[tile, :])
                    top = jnp.max(scores, axis=0, keepdims=True)
                    shift_ref[:, tile] = jnp.maximum(shift_ref[:, tile], top)
                return carry

            def again(block, carry):
                pltpu.sync_copy(p_any.at[rows_of(block, BLOCK)], p_buf)
                fill(p_buf, block)
                return carry

            blocks = total.shape[0]
            lax.fori_loop(0, blocks, peak, 0)
            lax.fori_loop(0, blocks, again, 0)

        found = jnp.sum(total[...], axis=0, keepdims=True)
        shift = shift_ref[...] * gain
        shift_ref[...] = shift
        lse_ref[...] = shift + jnp.log2(found)


def stats(place, own, e, p, gain):
    docs, width = e.shape
    protos = p.shape[0]
    blocks = protos // BLOCK
    return pl.pallas_call(
        functools.partial(stats_kernel, gain),
        grid_spec=pltpu.PrefetchScalarGridSpec(
            num_scalar_prefetch=1,
            grid=(blocks,),
            in_specs=[
                pl.BlockSpec((docs, width), lambda i, place: (0, 0)),
                pl.BlockSpec((BLOCK, width), lambda i, place: (i, 0)),
                pl.BlockSpec(memory_space=pl.ANY),
            ],
            out_specs=[whole()] * 4,
            scratch_shapes=[
                pltpu.VMEM((blocks, docs), F32),
                pltpu.VMEM((BLOCK, width), BF16),
            ],
        ),
        out_shape=[
            pltpu.VMEM((protos, docs), BF16),
            pltpu.VMEM((1, docs), F32),
            pltpu.VMEM((1, docs), F32),
            pltpu.VMEM((own, width), BF16),
        ],
        compiler_params=params(),
    )(place, e, p, p)


def split(x):
    high = x.astype(BF16)
    rest = x - high.astype(F32)
    mid = rest.astype(BF16)
    low = (rest - mid.astype(F32)).astype(BF16)
    return [part.astype(F32) for part in (high, mid, low)]


def columns_kernel(num_ref, w_ref, num_out, out_ref, turned):
    del num_out
    docs = num_ref.shape[1]
    taken = turned.shape[0]
    w = w_ref[...]
    rows = split(w[:, :taken]) + [jnp.zeros((CHUNK - 3, taken), F32)]
    turned[...] = jnp.concatenate(rows, axis=0).T.astype(BF16)
    lane = lax.broadcasted_iota(jnp.int32, out_ref.shape, 1)

    def body(group, found):
        base = pl.multiple_of(group * COLUMN_GROUP * CHUNK, CHUNK)
        part = jnp.dot(
            num_ref[pl.ds(base, COLUMN_GROUP * CHUNK), :taken],
            turned[...],
            preferred_element_type=F32,
        )
        for k in range(COLUMN_GROUP):
            here = part[k * CHUNK : (k + 1) * CHUNK]
            place = pl.ds(pl.multiple_of(base + k * CHUNK, CHUNK), CHUNK)
            for d in range(taken, docs, CHUNK):
                here += num_ref[place, d : d + CHUNK].astype(F32) * w[:, d : d + CHUNK]
            column = jnp.sum(here, axis=1, keepdims=True)
            found = jnp.where(lane == group * COLUMN_GROUP + k, column, found)
        return found

    groups = num_ref.shape[0] // (COLUMN_GROUP * CHUNK)
    out_ref[...] = lax.fori_loop(0, groups, body, jnp.ones(out_ref.shape, F32))


def chunk_lanes(protos):
    return -(-protos // (CHUNK * CHUNK)) * CHUNK


def columns(num, w):
    protos, docs = num.shape
    return pl.pallas_call(
        columns_kernel,
        in_specs=[whole()] * 2,
        out_specs=[whole()] * 2,
        out_shape=[pltpu.VMEM(num.shape, BF16), pltpu.VMEM((CHUNK, chunk_lanes(protos)), F32)],
        input_output_aliases={0: 0},
        scratch_shapes=[pltpu.VMEM((docs // 2, CHUNK), BF16)],
        compiler_params=params(),
    )(num, in_vmem(w))


def rows_kernel(num_ref, w_ref, cs_ref, num_out, out_ref, parts):
    del num_out
    docs = num_ref.shape[1]
    turned = cs_ref[...]
    for j, part in enumerate(split(turned.T)):
        parts[j] = part
    lane = lax.broadcasted_iota(jnp.int32, turned.shape, 1)

    def body(group, carry):
        added, product = carry
        base = pl.multiple_of(group * ROW_GROUP * CHUNK, CHUNK)
        rows = [
            jnp.concatenate(
                [parts[j, pl.ds(group * ROW_GROUP + k, 1), :] for k in range(ROW_TAKEN)], axis=1
            )
            for j in range(3)
        ]
        rows.append(jnp.zeros((5, ROW_TAKEN * CHUNK), F32))
        product = product + jnp.dot(
            jnp.concatenate(rows, axis=0).astype(BF16),
            num_ref[pl.ds(base, ROW_TAKEN * CHUNK), :],
            preferred_element_type=F32,
        )
        for k in range(ROW_TAKEN, ROW_GROUP):
            here = jnp.where(lane == group * ROW_GROUP + k, turned, 0.0)
            column = jnp.sum(here, axis=1, keepdims=True)
            place = pl.ds(pl.multiple_of(base + k * CHUNK, CHUNK), CHUNK)
            scaled = num_ref[place, :].astype(F32) * column
            added = added + jnp.sum(scaled.reshape(CHUNK // 8, 8, docs), axis=0)
        return added, product

    groups = num_ref.shape[0] // (ROW_GROUP * CHUNK)
    zero = jnp.zeros((8, docs), F32)
    added, product = lax.fori_loop(0, groups, body, (zero, zero))
    out_ref[...] = w_ref[...] * jnp.sum(added + product, axis=0, keepdims=True)


def row_sums(num, w, cs):
    docs = num.shape[1]
    return pl.pallas_call(
        rows_kernel,
        in_specs=[whole()] * 3,
        out_specs=[whole()] * 2,
        out_shape=[pltpu.VMEM(num.shape, BF16), pltpu.VMEM((1, docs), F32)],
        input_output_aliases={0: 0},
        scratch_shapes=[pltpu.VMEM((3, cs.shape[1], CHUNK), F32)],
        compiler_params=params(),
    )(num, in_vmem(w), in_vmem(cs))


def share_kernel(gain, e_ref, p_ref, x_ref, held_ref, num_ref, shift_ref, x_out, held_out):
    del held_ref, held_out

    @pl.when(pl.program_id(0) == 0)
    def _():
        x_out[...] = x_ref[...]

    first = transposed_dot(p_ref[:OWN_FIRST, :], e_ref[...])
    shift = jnp.max(first, axis=0, keepdims=True)
    num = jnp.exp2((transposed_dot(p_ref[...], e_ref[...]) - shift) * gain)
    num_ref[...] = num.astype(BF16)
    shift_ref[...] = shift * gain
    found = jnp.sum(num, axis=0, keepdims=True)
    fits = jnp.min(jnp.where(found < LARGE, 1.0, 0.0))

    @pl.when(fits < 0.5)
    def _():
        scores = transposed_dot(p_ref[...], e_ref[...])
        peak = jnp.max(scores, axis=0, keepdims=True)
        num_ref[...] = jnp.exp2((scores - peak) * gain).astype(BF16)
        shift_ref[...] = peak * gain


def share(e, p_own, x, held, gain):
    docs, width = e.shape
    own = p_own.shape[0]
    return pl.pallas_call(
        functools.partial(share_kernel, gain),
        grid=(docs // DOC_TILE,),
        in_specs=[pl.BlockSpec((DOC_TILE, width), lambda i: (i, 0))] + [whole()] * 3,
        out_specs=[
            pl.BlockSpec((own, DOC_TILE), lambda i: (0, i)),
            pl.BlockSpec((1, DOC_TILE), lambda i: (0, i)),
            whole(),
            whole(),
        ],
        out_shape=[
            pltpu.HBM((own, docs), BF16),
            pltpu.VMEM((1, docs), F32),
            pltpu.VMEM(x.shape, F32),
            pltpu.VMEM(held.shape, held.dtype),
        ],
        input_output_aliases={3: 3},
        compiler_params=params(),
    )(e, in_vmem(p_own), in_vmem(x), in_vmem(held))


def update_kernel(gain, place_ref, e_ref, v_ref, p_ref, cs_ref, *refs):
    nums, shifts = refs[:HELD], refs[HELD : 2 * HELD]
    out_ref, scores, acc, held, arrived = refs[2 * HELD :]
    step = pl.program_id(0)
    fresh = pl.num_programs(0) - HELD
    own = p_ref.shape[0]
    size = scores.shape[1]
    places = [slice(d, d + size) for d in range(0, own, size)]

    def add(place, part):
        acc[place, :] += jnp.dot(part.astype(BF16), e_ref[...], preferred_element_type=F32)

    @pl.when(step == 0)
    def _():
        acc[...] = jnp.zeros_like(acc)
        for k in range(HELD):
            pltpu.make_async_copy(nums[k], held.at[k], arrived.at[k]).start()

    for k in range(HELD):

        @pl.when(step == fresh + k)
        def _():
            pltpu.make_async_copy(nums[k], held.at[k], arrived.at[k]).wait()
            weight = jnp.exp2(shifts[k][...] + v_ref[...])
            for place in places:
                add(place, held[k, place, :].astype(F32) * weight)

    @pl.when(step < fresh)
    def _():
        def score(j):
            scores[j % 2] = transposed_dot(p_ref[places[j], :], e_ref[...])

        score(0)
        for j in range(len(places)):
            if j + 1 < len(places):
                score(j + 1)
            add(places[j], jnp.exp2(scores[j % 2] * gain + v_ref[...]))

    @pl.when(step == pl.num_programs(0) - 1)
    def _():
        lane = lax.broadcasted_iota(jnp.int32, cs_ref.shape, 1)
        chunks = own // CHUNK
        for k in range(chunks):
            here = jnp.where(lane == place_ref[0] * chunks + k, cs_ref[...], 0.0)
            place = slice(k * CHUNK, (k + 1) * CHUNK)
            summed = acc[place, :] * jnp.sum(here, axis=1, keepdims=True)
            square = jnp.mean(summed * summed, axis=1, keepdims=True)
            out_ref[place, :] = (summed * lax.rsqrt(square + 1e-06)).astype(BF16)


def update(place, docs, e_all, v, p_own, cs, nums, shifts, gain):
    own, width = p_own.shape
    size = min(UPDATE_ROWS, own)
    ranks = e_all.shape[0] // docs

    def turn(i):
        return lax.rem(i + HELD, ranks)

    return pl.pallas_call(
        functools.partial(update_kernel, gain),
        grid_spec=pltpu.PrefetchScalarGridSpec(
            num_scalar_prefetch=1,
            grid=(ranks,),
            in_specs=[
                pl.BlockSpec(
                    (docs, width), lambda i, place: (jnp.bitwise_xor(place[0], turn(i)), 0)
                ),
                pl.BlockSpec((1, docs), lambda i, place: (0, turn(i))),
            ]
            + [whole()] * 2
            + [pl.BlockSpec(memory_space=pl.ANY)] * HELD
            + [whole()] * HELD,
            out_specs=pl.BlockSpec((own, width), lambda i, place: (0, 0)),
            scratch_shapes=[
                pltpu.VMEM((2, size, docs), F32),
                pltpu.VMEM((own, width), F32),
                pltpu.VMEM((HELD, own, docs), BF16),
                pltpu.SemaphoreType.DMA((HELD,)),
            ],
        ),
        out_shape=jax.ShapeDtypeStruct((own, width), BF16),
        compiler_params=params(),
    )(
        place,
        in_hbm(e_all),
        v,
        in_vmem(p_own),
        in_vmem(cs),
        *[in_hbm(num) for num in nums],
        *[in_vmem(shift) for shift in shifts],
    )


def swap(x, axis, bit):
    size = lax.axis_size(axis)
    return lax.ppermute(x, axis, [(i, i ^ bit) for i in range(size)])


def bits(axis):
    bit = 1
    while bit < lax.axis_size(axis):
        yield bit
        bit *= 2


def reduce_over(x, axis, combine, jobs={}):
    for bit in bits(axis):
        other = swap(x, axis, bit)
        for job in jobs.get(bit, ()):
            x = job(x)
        x = combine(x, other)
    return x


def gather_over(x, axis, jobs={}):
    for bit in bits(axis):
        other = swap(x, axis, bit)
        for job in jobs.get(bit, ()):
            x = job(x)
        x = jnp.concatenate([x, other], axis=1)
    return x


def log_add(a, b):
    top = jnp.maximum(a, b)
    return top + jnp.log2(jnp.exp2(a - top) + jnp.exp2(b - top))


def on_device(embeddings, prototypes):
    docs, width = embeddings.shape
    protos = prototypes.shape[0]
    doc_ranks = lax.axis_size("docs")
    total_docs = docs * doc_ranks
    total_protos = protos * lax.axis_size("protos")
    own = protos // doc_ranks
    gain = 4.0 / math.sqrt(width) / math.log(2.0)

    place = lax.axis_index("docs").astype(jnp.int32)

    e_all = lax.all_gather(embeddings, "docs", tiled=True)
    partner = swap(embeddings, "docs", 1)
    state = {}
    nums, shifts = [None] * HELD, [None] * HELD

    def share_job(k):
        def job(x):
            e = in_hbm((embeddings, partner)[k])
            nums[k], shifts[k], x, state["num"] = share(e, state["own"], x, state["num"], gain)
            return x

        return job

    doc_bits = list(bits("docs"))
    early = {doc_bits[1]: [share_job(0)], doc_bits[2]: [share_job(1)]}

    num, shift, lse, own_table = stats(
        place.reshape(1), own, in_hbm(embeddings), in_hbm(prototypes), gain
    )
    state["own"], state["num"] = own_table, num
    lse = reduce_over(lse, "protos", log_add)
    w = jnp.exp2(shift - lse)
    weight = w
    for sweep_index in range(SWEEPS):
        beside = early if sweep_index == 0 else {}
        state["num"], col_local = columns(in_vmem(state["num"]), weight)
        col_total = reduce_over(col_local, "docs", jnp.add, beside)
        cs = 1.0 / (total_protos * col_total)
        state["num"], row_local = row_sums(in_vmem(state["num"]), w, cs)
        row_sum = reduce_over(row_local, "protos", jnp.add)
        r = 1.0 / (total_docs * row_sum)
        weight = w * r
    v = gather_over(jnp.log2(r * total_docs) - lse, "docs")
    new_prototypes = update(
        place.reshape(1), docs, e_all, v, state["own"], cs, nums, shifts, gain
    )
    column_potential = jnp.log(total_docs * cs.T.reshape(-1)[:protos])
    row_potential = jnp.log(lax.optimization_barrier(r)).reshape(-1)
    return (new_prototypes, column_potential, row_potential)


def solution(mesh):
    placed = (P("docs", None), P("protos", None))
    return jax.shard_map(
        on_device,
        mesh=mesh,
        in_specs=placed,
        out_specs=(P(("protos", "docs"), None), P("protos"), P("docs")),
        check_vma=False,
    )
```

```python
import functools
import math

import jax
import jax.numpy as jnp
from jax import lax
from jax.experimental import pallas as pl
from jax.experimental.pallas import tpu as pltpu
from jax.sharding import PartitionSpec as P

SWEEPS = 2
VMEM_LIMIT = 26 << 20
BLOCK = 1024
FIRST = 256
DOC_TILE = 256
LARGE = 2.0**60
CHUNK = 128
COLUMN_GROUP = 32
ROW_GROUP = 16
ROW_TAKEN = 10
OWN_FIRST = 128
UPDATE_ROWS = 512
HELD = 2
F32 = jnp.float32
BF16 = jnp.bfloat16


def params():
    return pltpu.CompilerParams(vmem_limit_bytes=VMEM_LIMIT)


def whole():
    return pl.BlockSpec(memory_space=pltpu.VMEM)


def in_vmem(x):
    return pltpu.with_memory_space_constraint(x, pltpu.VMEM)


def in_hbm(x):
    return pltpu.with_memory_space_constraint(x, pltpu.HBM)


def transposed_dot(a, b):
    return lax.dot_general(a, b, (((1,), (1,)), ((), ())), preferred_element_type=F32)


def rows_of(index, size):
    return pl.ds(pl.multiple_of(index * size, size), size)


def stats_kernel(gain, place_ref, e_ref, p_ref, p_any, num_ref, shift_ref, lse_ref, own_ref, total, p_buf):
    step = pl.program_id(0)
    docs = e_ref.shape[0]
    tiles = [slice(d, d + DOC_TILE) for d in range(0, docs, DOC_TILE)]

    @pl.when(step == 0)
    def _():
        first = transposed_dot(p_ref[:FIRST, :], e_ref[...])
        shift_ref[...] = jnp.max(first, axis=0, keepdims=True)

    def fill(block_ref, block):
        sums = []
        for tile in tiles:
            scores = transposed_dot(block_ref[...], e_ref[tile, :])
            num = jnp.exp2((scores - shift_ref[:, tile]) * gain)
            num_ref[rows_of(block, BLOCK), tile] = num.astype(BF16)
            sums.append(jnp.sum(num, axis=0, keepdims=True))
        total[pl.ds(block, 1), :] = jnp.concatenate(sums, axis=1)

    fill(p_ref, step)
    own = own_ref.shape[0]
    count, per = max(own // BLOCK, 1), max(BLOCK // own, 1)
    for j in range(count):

        @pl.when(step == place_ref[0] * count // per + j)
        def _():
            offset = pl.multiple_of((place_ref[0] % per) * own, 16) if per > 1 else 0
            size = min(own, BLOCK)
            own_ref[j * size : (j + 1) * size, :] = p_ref[pl.ds(offset, size), :]

    @pl.when(step == pl.num_programs(0) - 1)
    def _():
        found = jnp.sum(total[...], axis=0, keepdims=True)
        fits = jnp.min(jnp.where(found < LARGE, 1.0, 0.0))

        @pl.when(fits < 0.5)
        def _():
            def peak(block, carry):
                pltpu.sync_copy(p_any.at[rows_of(block, BLOCK)], p_buf)
                for tile in tiles:
                    scores = transposed_dot(p_buf[...], e_ref[tile, :])
                    top = jnp.max(scores, axis=0, keepdims=True)
                    shift_ref[:, tile] = jnp.maximum(shift_ref[:, tile], top)
                return carry

            def again(block, carry):
                pltpu.sync_copy(p_any.at[rows_of(block, BLOCK)], p_buf)
                fill(p_buf, block)
                return carry

            blocks = total.shape[0]
            lax.fori_loop(0, blocks, peak, 0)
            lax.fori_loop(0, blocks, again, 0)

        found = jnp.sum(total[...], axis=0, keepdims=True)
        shift = shift_ref[...] * gain
        shift_ref[...] = shift
        lse_ref[...] = shift + jnp.log2(found)


def stats(place, own, e, p, gain):
    docs, width = e.shape
    protos = p.shape[0]
    blocks = protos // BLOCK
    return pl.pallas_call(
        functools.partial(stats_kernel, gain),
        grid_spec=pltpu.PrefetchScalarGridSpec(
            num_scalar_prefetch=1,
            grid=(blocks,),
            in_specs=[
                pl.BlockSpec((docs, width), lambda i, place: (0, 0)),
                pl.BlockSpec((BLOCK, width), lambda i, place: (i, 0)),
                pl.BlockSpec(memory_space=pl.ANY),
            ],
            out_specs=[whole()] * 4,
            scratch_shapes=[
                pltpu.VMEM((blocks, docs), F32),
                pltpu.VMEM((BLOCK, width), BF16),
            ],
        ),
        out_shape=[
            pltpu.VMEM((protos, docs), BF16),
            pltpu.VMEM((1, docs), F32),
            pltpu.VMEM((1, docs), F32),
            pltpu.VMEM((own, width), BF16),
        ],
        compiler_params=params(),
    )(place, e, p, p)


def split(x):
    high = x.astype(BF16)
    rest = x - high.astype(F32)
    mid = rest.astype(BF16)
    low = (rest - mid.astype(F32)).astype(BF16)
    return [part.astype(F32) for part in (high, mid, low)]


def halves(place_ref):
    core = lax.rem(place_ref[0], 2)
    return rows_of(core, CHUNK // 2), rows_of(1 - core, CHUNK // 2)


def columns_kernel(num_ref, w_ref, place_ref, num_out, mine_ref, other_ref, turned, sums):
    del num_out
    docs = num_ref.shape[1]
    taken = turned.shape[0]
    w = w_ref[...]
    rows = split(w[:, :taken]) + [jnp.zeros((CHUNK - 3, taken), F32)]
    turned[...] = jnp.concatenate(rows, axis=0).T.astype(BF16)
    lane = lax.broadcasted_iota(jnp.int32, sums.shape, 1)

    def body(group, found):
        base = pl.multiple_of(group * COLUMN_GROUP * CHUNK, CHUNK)
        part = jnp.dot(
            num_ref[pl.ds(base, COLUMN_GROUP * CHUNK), :taken],
            turned[...],
            preferred_element_type=F32,
        )
        for k in range(COLUMN_GROUP):
            here = part[k * CHUNK : (k + 1) * CHUNK]
            place = pl.ds(pl.multiple_of(base + k * CHUNK, CHUNK), CHUNK)
            for d in range(taken, docs, CHUNK):
                here += num_ref[place, d : d + CHUNK].astype(F32) * w[:, d : d + CHUNK]
            column = jnp.sum(here, axis=1, keepdims=True)
            found = jnp.where(lane == group * COLUMN_GROUP + k, column, found)
        return found

    groups = num_ref.shape[0] // (COLUMN_GROUP * CHUNK)
    sums[...] = lax.fori_loop(0, groups, body, jnp.ones(sums.shape, F32))
    mine, other = halves(place_ref)
    mine_ref[...] = sums[mine, :]
    other_ref[...] = sums[other, :]


def chunk_lanes(protos):
    return -(-protos // (CHUNK * CHUNK)) * CHUNK


def columns(num, w, place):
    protos, docs = num.shape
    lanes = chunk_lanes(protos)
    return pl.pallas_call(
        columns_kernel,
        in_specs=[whole()] * 2 + [pl.BlockSpec(memory_space=pltpu.SMEM)],
        out_specs=[whole()] * 3,
        out_shape=[pltpu.VMEM(num.shape, BF16)] + [pltpu.VMEM((CHUNK // 2, lanes), F32)] * 2,
        input_output_aliases={0: 0},
        scratch_shapes=[pltpu.VMEM((docs // 2, CHUNK), BF16), pltpu.VMEM((CHUNK, lanes), F32)],
        compiler_params=params(),
    )(num, in_vmem(w), place)


def rows_kernel(total, num_ref, w_ref, mine_ref, other_ref, place_ref, num_out, out_ref, cs_ref, *refs):
    del num_out
    parts = refs[-1]
    copy = None
    if len(refs) > 1:
        taken, done = refs[0], refs[1]
        own = taken.shape[0]
        copy = pltpu.make_async_copy(num_ref.at[rows_of(place_ref[0], own)], taken, done)
        copy.start()
    docs = num_ref.shape[1]
    mine, other = halves(place_ref)
    cs_ref[mine, :] = 1.0 / (total * mine_ref[...])
    cs_ref[other, :] = 1.0 / (total * other_ref[...])
    turned = cs_ref[...]
    for j, part in enumerate(split(turned.T)):
        parts[j] = part
    lane = lax.broadcasted_iota(jnp.int32, turned.shape, 1)

    def body(group, carry):
        added, product = carry
        base = pl.multiple_of(group * ROW_GROUP * CHUNK, CHUNK)
        rows = [
            jnp.concatenate(
                [parts[j, pl.ds(group * ROW_GROUP + k, 1), :] for k in range(ROW_TAKEN)], axis=1
            )
            for j in range(3)
        ]
        rows.append(jnp.zeros((5, ROW_TAKEN * CHUNK), F32))
        product = product + jnp.dot(
            jnp.concatenate(rows, axis=0).astype(BF16),
            num_ref[pl.ds(base, ROW_TAKEN * CHUNK), :],
            preferred_element_type=F32,
        )
        for k in range(ROW_TAKEN, ROW_GROUP):
            here = jnp.where(lane == group * ROW_GROUP + k, turned, 0.0)
            column = jnp.sum(here, axis=1, keepdims=True)
            place = pl.ds(pl.multiple_of(base + k * CHUNK, CHUNK), CHUNK)
            scaled = num_ref[place, :].astype(F32) * column
            added = added + jnp.sum(scaled.reshape(CHUNK // 8, 8, docs), axis=0)
        return added, product

    groups = num_ref.shape[0] // (ROW_GROUP * CHUNK)
    zero = jnp.zeros((8, docs), F32)
    added, product = lax.fori_loop(0, groups, body, (zero, zero))
    out_ref[...] = w_ref[...] * jnp.sum(added + product, axis=0, keepdims=True)
    if copy is not None:
        copy.wait()


def row_sums(num, w, mine, other, place, total, own):
    docs = num.shape[1]
    lanes = mine.shape[1]
    return pl.pallas_call(
        functools.partial(rows_kernel, total),
        in_specs=[whole()] * 4 + [pl.BlockSpec(memory_space=pltpu.SMEM)],
        out_specs=[whole()] * 3 + [pl.BlockSpec(memory_space=pl.ANY)] * (own > 0),
        out_shape=[
            pltpu.VMEM(num.shape, BF16),
            pltpu.VMEM((1, docs), F32),
            pltpu.VMEM((CHUNK, lanes), F32),
        ]
        + [pltpu.HBM((own, docs), BF16)] * (own > 0),
        input_output_aliases={0: 0},
        scratch_shapes=[pltpu.SemaphoreType.DMA] * (own > 0) + [pltpu.VMEM((3, lanes, CHUNK), F32)],
        compiler_params=params(),
    )(num, in_vmem(w), in_vmem(mine), in_vmem(other), place)


def share_kernel(gain, e_ref, p_ref, x_ref, held_ref, num_ref, shift_ref, x_out, held_out):
    del held_ref, held_out

    @pl.when(pl.program_id(0) == 0)
    def _():
        x_out[...] = x_ref[...]

    first = transposed_dot(p_ref[:OWN_FIRST, :], e_ref[...])
    shift = jnp.max(first, axis=0, keepdims=True)
    num = jnp.exp2((transposed_dot(p_ref[...], e_ref[...]) - shift) * gain)
    num_ref[...] = num.astype(BF16)
    shift_ref[...] = shift * gain
    found = jnp.sum(num, axis=0, keepdims=True)
    fits = jnp.min(jnp.where(found < LARGE, 1.0, 0.0))

    @pl.when(fits < 0.5)
    def _():
        scores = transposed_dot(p_ref[...], e_ref[...])
        peak = jnp.max(scores, axis=0, keepdims=True)
        num_ref[...] = jnp.exp2((scores - peak) * gain).astype(BF16)
        shift_ref[...] = peak * gain


def share(e, p_own, x, held, gain):
    docs, width = e.shape
    own = p_own.shape[0]
    return pl.pallas_call(
        functools.partial(share_kernel, gain),
        grid=(docs // DOC_TILE,),
        in_specs=[pl.BlockSpec((DOC_TILE, width), lambda i: (i, 0))] + [whole()] * 3,
        out_specs=[
            pl.BlockSpec((own, DOC_TILE), lambda i: (0, i)),
            pl.BlockSpec((1, DOC_TILE), lambda i: (0, i)),
            whole(),
            whole(),
        ],
        out_shape=[
            pltpu.HBM((own, docs), BF16),
            pltpu.VMEM((1, docs), F32),
            pltpu.VMEM(x.shape, F32),
            pltpu.VMEM(held.shape, held.dtype),
        ],
        input_output_aliases={3: 3},
        compiler_params=params(),
    )(e, in_vmem(p_own), in_vmem(x), in_vmem(held))


def update_kernel(gain, place_ref, e_ref, v_ref, p_ref, cs_ref, *refs):
    nums, shifts = refs[:HELD], refs[HELD : 2 * HELD]
    out_ref, scores, acc, held, arrived = refs[2 * HELD :]
    step = pl.program_id(0)
    fresh = pl.num_programs(0) - HELD
    own = p_ref.shape[0]
    size = scores.shape[1]
    places = [slice(d, d + size) for d in range(0, own, size)]

    def add(place, part):
        acc[place, :] += jnp.dot(part.astype(BF16), e_ref[...], preferred_element_type=F32)

    @pl.when(step == 0)
    def _():
        acc[...] = jnp.zeros_like(acc)
        for k in range(HELD):
            pltpu.make_async_copy(nums[k], held.at[k], arrived.at[k]).start()

    for k in range(HELD):

        @pl.when(step == fresh + k)
        def _():
            pltpu.make_async_copy(nums[k], held.at[k], arrived.at[k]).wait()
            weight = jnp.exp2(shifts[k][...] + v_ref[...])
            for place in places:
                add(place, held[k, place, :].astype(F32) * weight)

    @pl.when(step < fresh)
    def _():
        def score(j):
            scores[j % 2] = transposed_dot(p_ref[places[j], :], e_ref[...])

        score(0)
        for j in range(len(places)):
            if j + 1 < len(places):
                score(j + 1)
            add(places[j], jnp.exp2(scores[j % 2] * gain + v_ref[...]))

    @pl.when(step == pl.num_programs(0) - 1)
    def _():
        lane = lax.broadcasted_iota(jnp.int32, cs_ref.shape, 1)
        chunks = own // CHUNK
        for k in range(chunks):
            here = jnp.where(lane == place_ref[0] * chunks + k, cs_ref[...], 0.0)
            place = slice(k * CHUNK, (k + 1) * CHUNK)
            summed = acc[place, :] * jnp.sum(here, axis=1, keepdims=True)
            square = jnp.mean(summed * summed, axis=1, keepdims=True)
            out_ref[place, :] = (summed * lax.rsqrt(square + 1e-06)).astype(BF16)


def update(place, docs, e_all, v, p_own, cs, nums, shifts, gain):
    own, width = p_own.shape
    size = min(UPDATE_ROWS, own)
    ranks = e_all.shape[0] // docs

    def turn(i):
        return lax.rem(i + HELD, ranks)

    return pl.pallas_call(
        functools.partial(update_kernel, gain),
        grid_spec=pltpu.PrefetchScalarGridSpec(
            num_scalar_prefetch=1,
            grid=(ranks,),
            in_specs=[
                pl.BlockSpec(
                    (docs, width), lambda i, place: (jnp.bitwise_xor(place[0], turn(i)), 0)
                ),
                pl.BlockSpec((1, docs), lambda i, place: (0, turn(i))),
            ]
            + [whole()] * 2
            + [pl.BlockSpec(memory_space=pl.ANY)] * HELD
            + [whole()] * HELD,
            out_specs=pl.BlockSpec((own, width), lambda i, place: (0, 0)),
            scratch_shapes=[
                pltpu.VMEM((2, size, docs), F32),
                pltpu.VMEM((own, width), F32),
                pltpu.VMEM((HELD, own, docs), BF16),
                pltpu.SemaphoreType.DMA((HELD,)),
            ],
        ),
        out_shape=jax.ShapeDtypeStruct((own, width), BF16),
        compiler_params=params(),
    )(
        place,
        in_hbm(e_all),
        v,
        in_vmem(p_own),
        in_vmem(cs),
        *[in_hbm(num) for num in nums],
        *[in_vmem(shift) for shift in shifts],
    )


def swap(x, axis, bit):
    size = lax.axis_size(axis)
    return lax.ppermute(x, axis, [(i, i ^ bit) for i in range(size)])


def bits(axis):
    bit = 1
    while bit < lax.axis_size(axis):
        yield bit
        bit *= 2


def reduce_over(x, axis, combine):
    for bit in bits(axis):
        x = combine(x, swap(x, axis, bit))
    return x


def gather_over(x, axis):
    for bit in bits(axis):
        x = jnp.concatenate([x, swap(x, axis, bit)], axis=1)
    return x


def sum_over_docs(mine, other, jobs={}):
    mine = mine + swap(other, "docs", 1)
    for bit in list(bits("docs"))[1:]:
        arrived = swap(mine, "docs", bit)
        for job in jobs.get(bit, ()):
            mine = job(mine)
        mine = mine + arrived
    return mine, swap(mine, "docs", 1)


def log_add(a, b):
    top = jnp.maximum(a, b)
    return top + jnp.log2(jnp.exp2(a - top) + jnp.exp2(b - top))


def on_device(embeddings, prototypes):
    docs, width = embeddings.shape
    protos = prototypes.shape[0]
    doc_ranks = lax.axis_size("docs")
    total_docs = docs * doc_ranks
    total_protos = protos * lax.axis_size("protos")
    own = protos // doc_ranks
    gain = 4.0 / math.sqrt(width) / math.log(2.0)

    place = lax.axis_index("docs").astype(jnp.int32)

    e_all = lax.all_gather(embeddings, "docs", tiled=True)
    partner = swap(embeddings, "docs", 1)
    state = {}
    nums, shifts = [None] * HELD, [None] * HELD

    def share_job(k):
        def job(x):
            e = in_hbm(partner)
            nums[k], shifts[k], x, state["num"] = share(e, state["own"], x, state["num"], gain)
            return x

        return job

    doc_bits = list(bits("docs"))
    early = {doc_bits[1]: [share_job(1)]}

    num, shift, lse, own_table = stats(
        place.reshape(1), own, in_hbm(embeddings), in_hbm(prototypes), gain
    )
    state["own"], state["num"] = own_table, num
    lse = reduce_over(lse, "protos", log_add)
    w = jnp.exp2(shift - lse)
    weight = w
    for sweep_index in range(SWEEPS):
        beside = early if sweep_index == 0 else {}
        state["num"], *parts = columns(in_vmem(state["num"]), weight, place.reshape(1))
        mine, other = sum_over_docs(*parts, beside)
        state["num"], row_local, cs, *taken = row_sums(
            in_vmem(state["num"]),
            w,
            mine,
            other,
            place.reshape(1),
            float(total_protos),
            0 if sweep_index else own,
        )
        if taken:
            nums[0], shifts[0] = taken[0], shift
        row_sum = reduce_over(row_local, "protos", jnp.add)
        r = 1.0 / (total_docs * row_sum)
        weight = w * r
    v = gather_over(jnp.log2(r * total_docs) - lse, "docs")
    new_prototypes = update(
        place.reshape(1), docs, e_all, v, state["own"], cs, nums, shifts, gain
    )
    column_potential = jnp.log(total_docs * cs.T.reshape(-1)[:protos])
    row_potential = jnp.log(lax.optimization_barrier(r)).reshape(-1)
    return (new_prototypes, column_potential, row_potential)


def solution(mesh):
    placed = (P("docs", None), P("protos", None))
    return jax.shard_map(
        on_device,
        mesh=mesh,
        in_specs=placed,
        out_specs=(P(("protos", "docs"), None), P("protos"), P("docs")),
        check_vma=False,
    )
```

```python
import functools
import math

import jax
import jax.numpy as jnp
from jax import lax
from jax.experimental import pallas as pl
from jax.experimental.pallas import tpu as pltpu
from jax.sharding import PartitionSpec as P

SWEEPS = 2
VMEM_LIMIT = 26 << 20
BLOCK = 1024
FIRST = 256
DOC_TILE = 256
LARGE = 2.0**60
CHUNK = 128
COLUMN_GROUP = 32
ROW_GROUP = 16
ROW_TAKEN = 10
OWN_FIRST = 128
UPDATE_ROWS = 512
HELD = 2
F32 = jnp.float32
BF16 = jnp.bfloat16


def params():
    return pltpu.CompilerParams(vmem_limit_bytes=VMEM_LIMIT)


def whole():
    return pl.BlockSpec(memory_space=pltpu.VMEM)


def in_vmem(x):
    return pltpu.with_memory_space_constraint(x, pltpu.VMEM)


def in_hbm(x):
    return pltpu.with_memory_space_constraint(x, pltpu.HBM)


def transposed_dot(a, b):
    return lax.dot_general(a, b, (((1,), (1,)), ((), ())), preferred_element_type=F32)


def rows_of(index, size):
    return pl.ds(pl.multiple_of(index * size, size), size)


def stats_kernel(gain, place_ref, e_ref, p_ref, p_any, num_ref, shift_ref, lse_ref, own_ref, total, p_buf):
    step = pl.program_id(0)
    docs = e_ref.shape[0]
    tiles = [slice(d, d + DOC_TILE) for d in range(0, docs, DOC_TILE)]

    @pl.when(step == 0)
    def _():
        first = transposed_dot(p_ref[:FIRST, :], e_ref[...])
        shift_ref[...] = jnp.max(first, axis=0, keepdims=True)

    def fill(block_ref, block):
        sums = []
        for tile in tiles:
            scores = transposed_dot(block_ref[...], e_ref[tile, :])
            num = jnp.exp2((scores - shift_ref[:, tile]) * gain)
            num_ref[rows_of(block, BLOCK), tile] = num.astype(BF16)
            sums.append(jnp.sum(num, axis=0, keepdims=True))
        total[pl.ds(block, 1), :] = jnp.concatenate(sums, axis=1)

    fill(p_ref, step)
    own = own_ref.shape[0]
    count, per = max(own // BLOCK, 1), max(BLOCK // own, 1)
    for j in range(count):

        @pl.when(step == place_ref[0] * count // per + j)
        def _():
            offset = pl.multiple_of((place_ref[0] % per) * own, 16) if per > 1 else 0
            size = min(own, BLOCK)
            own_ref[j * size : (j + 1) * size, :] = p_ref[pl.ds(offset, size), :]

    @pl.when(step == pl.num_programs(0) - 1)
    def _():
        found = jnp.sum(total[...], axis=0, keepdims=True)
        fits = jnp.min(jnp.where(found < LARGE, 1.0, 0.0))

        @pl.when(fits < 0.5)
        def _():
            def peak(block, carry):
                pltpu.sync_copy(p_any.at[rows_of(block, BLOCK)], p_buf)
                for tile in tiles:
                    scores = transposed_dot(p_buf[...], e_ref[tile, :])
                    top = jnp.max(scores, axis=0, keepdims=True)
                    shift_ref[:, tile] = jnp.maximum(shift_ref[:, tile], top)
                return carry

            def again(block, carry):
                pltpu.sync_copy(p_any.at[rows_of(block, BLOCK)], p_buf)
                fill(p_buf, block)
                return carry

            blocks = total.shape[0]
            lax.fori_loop(0, blocks, peak, 0)
            lax.fori_loop(0, blocks, again, 0)

        found = jnp.sum(total[...], axis=0, keepdims=True)
        shift = shift_ref[...] * gain
        shift_ref[...] = shift
        lse_ref[...] = shift + jnp.log2(found)


def stats(place, own, e, p, gain):
    docs, width = e.shape
    protos = p.shape[0]
    blocks = protos // BLOCK
    return pl.pallas_call(
        functools.partial(stats_kernel, gain),
        grid_spec=pltpu.PrefetchScalarGridSpec(
            num_scalar_prefetch=1,
            grid=(blocks,),
            in_specs=[
                pl.BlockSpec((docs, width), lambda i, place: (0, 0)),
                pl.BlockSpec((BLOCK, width), lambda i, place: (i, 0)),
                pl.BlockSpec(memory_space=pl.ANY),
            ],
            out_specs=[whole()] * 4,
            scratch_shapes=[
                pltpu.VMEM((blocks, docs), F32),
                pltpu.VMEM((BLOCK, width), BF16),
            ],
        ),
        out_shape=[
            pltpu.VMEM((protos, docs), BF16),
            pltpu.VMEM((1, docs), F32),
            pltpu.VMEM((1, docs), F32),
            pltpu.VMEM((own, width), BF16),
        ],
        compiler_params=params(),
    )(place, e, p, p)


def split(x):
    high = x.astype(BF16)
    rest = x - high.astype(F32)
    mid = rest.astype(BF16)
    low = (rest - mid.astype(F32)).astype(BF16)
    return [part.astype(F32) for part in (high, mid, low)]


def halves(place_ref):
    core = lax.rem(place_ref[0], 2)
    return rows_of(core, CHUNK // 2), rows_of(1 - core, CHUNK // 2)


def columns_kernel(num_ref, w_ref, place_ref, num_out, mine_ref, other_ref, turned, sums):
    del num_out
    docs = num_ref.shape[1]
    taken = turned.shape[0]
    w = w_ref[...]
    rows = split(w[:, :taken]) + [jnp.zeros((CHUNK - 3, taken), F32)]
    turned[...] = jnp.concatenate(rows, axis=0).T.astype(BF16)
    lane = lax.broadcasted_iota(jnp.int32, sums.shape, 1)

    def body(group, found):
        base = pl.multiple_of(group * COLUMN_GROUP * CHUNK, CHUNK)
        part = jnp.dot(
            num_ref[pl.ds(base, COLUMN_GROUP * CHUNK), :taken],
            turned[...],
            preferred_element_type=F32,
        )
        for k in range(COLUMN_GROUP):
            here = part[k * CHUNK : (k + 1) * CHUNK]
            place = pl.ds(pl.multiple_of(base + k * CHUNK, CHUNK), CHUNK)
            for d in range(taken, docs, CHUNK):
                here += num_ref[place, d : d + CHUNK].astype(F32) * w[:, d : d + CHUNK]
            column = jnp.sum(here, axis=1, keepdims=True)
            found = jnp.where(lane == group * COLUMN_GROUP + k, column, found)
        return found

    groups = num_ref.shape[0] // (COLUMN_GROUP * CHUNK)
    sums[...] = lax.fori_loop(0, groups, body, jnp.ones(sums.shape, F32))
    mine, other = halves(place_ref)
    mine_ref[...] = sums[mine, :]
    other_ref[...] = sums[other, :]


def chunk_lanes(protos):
    return -(-protos // (CHUNK * CHUNK)) * CHUNK


def columns(num, w, place):
    protos, docs = num.shape
    lanes = chunk_lanes(protos)
    return pl.pallas_call(
        columns_kernel,
        in_specs=[whole()] * 2 + [pl.BlockSpec(memory_space=pltpu.SMEM)],
        out_specs=[whole()] * 3,
        out_shape=[pltpu.VMEM(num.shape, BF16)] + [pltpu.VMEM((CHUNK // 2, lanes), F32)] * 2,
        input_output_aliases={0: 0},
        scratch_shapes=[pltpu.VMEM((docs // 2, CHUNK), BF16), pltpu.VMEM((CHUNK, lanes), F32)],
        compiler_params=params(),
    )(num, in_vmem(w), place)


def rows_kernel(total, num_ref, w_ref, mine_ref, other_ref, place_ref, num_out, out_ref, cs_ref, *refs):
    del num_out
    parts = refs[-1]
    copy = None
    if len(refs) > 1:
        taken, done = refs[0], refs[1]
        own = taken.shape[0]
        copy = pltpu.make_async_copy(num_ref.at[rows_of(place_ref[0], own)], taken, done)
        copy.start()
    docs = num_ref.shape[1]
    mine, other = halves(place_ref)
    cs_ref[mine, :] = 1.0 / (total * mine_ref[...])
    cs_ref[other, :] = 1.0 / (total * other_ref[...])
    turned = cs_ref[...]
    for j, part in enumerate(split(turned.T)):
        parts[j] = part
    lane = lax.broadcasted_iota(jnp.int32, turned.shape, 1)

    def body(group, carry):
        added, product = carry
        base = pl.multiple_of(group * ROW_GROUP * CHUNK, CHUNK)
        rows = [
            jnp.concatenate(
                [parts[j, pl.ds(group * ROW_GROUP + k, 1), :] for k in range(ROW_TAKEN)], axis=1
            )
            for j in range(3)
        ]
        rows.append(jnp.zeros((5, ROW_TAKEN * CHUNK), F32))
        product = product + jnp.dot(
            jnp.concatenate(rows, axis=0).astype(BF16),
            num_ref[pl.ds(base, ROW_TAKEN * CHUNK), :],
            preferred_element_type=F32,
        )
        for k in range(ROW_TAKEN, ROW_GROUP):
            here = jnp.where(lane == group * ROW_GROUP + k, turned, 0.0)
            column = jnp.sum(here, axis=1, keepdims=True)
            place = pl.ds(pl.multiple_of(base + k * CHUNK, CHUNK), CHUNK)
            scaled = num_ref[place, :].astype(F32) * column
            added = added + jnp.sum(scaled.reshape(CHUNK // 8, 8, docs), axis=0)
        return added, product

    groups = num_ref.shape[0] // (ROW_GROUP * CHUNK)
    zero = jnp.zeros((8, docs), F32)
    added, product = lax.fori_loop(0, groups, body, (zero, zero))
    out_ref[...] = w_ref[...] * jnp.sum(added + product, axis=0, keepdims=True)
    if copy is not None:
        copy.wait()


def row_sums(num, w, mine, other, place, total, own):
    docs = num.shape[1]
    lanes = mine.shape[1]
    return pl.pallas_call(
        functools.partial(rows_kernel, total),
        in_specs=[whole()] * 4 + [pl.BlockSpec(memory_space=pltpu.SMEM)],
        out_specs=[whole()] * 3 + [pl.BlockSpec(memory_space=pl.ANY)] * (own > 0),
        out_shape=[
            pltpu.VMEM(num.shape, BF16),
            pltpu.VMEM((1, docs), F32),
            pltpu.VMEM((CHUNK, lanes), F32),
        ]
        + [pltpu.HBM((own, docs), BF16)] * (own > 0),
        input_output_aliases={0: 0},
        scratch_shapes=[pltpu.SemaphoreType.DMA] * (own > 0) + [pltpu.VMEM((3, lanes, CHUNK), F32)],
        compiler_params=params(),
    )(num, in_vmem(w), in_vmem(mine), in_vmem(other), place)


def share_kernel(gain, e_ref, p_ref, x_ref, held_ref, num_ref, shift_ref, x_out, held_out):
    del held_ref, held_out

    @pl.when(pl.program_id(0) == 0)
    def _():
        x_out[...] = x_ref[...]

    first = transposed_dot(p_ref[:OWN_FIRST, :], e_ref[...])
    shift = jnp.max(first, axis=0, keepdims=True)
    num = jnp.exp2((transposed_dot(p_ref[...], e_ref[...]) - shift) * gain)
    num_ref[...] = num.astype(BF16)
    shift_ref[...] = shift * gain
    found = jnp.sum(num, axis=0, keepdims=True)
    fits = jnp.min(jnp.where(found < LARGE, 1.0, 0.0))

    @pl.when(fits < 0.5)
    def _():
        scores = transposed_dot(p_ref[...], e_ref[...])
        peak = jnp.max(scores, axis=0, keepdims=True)
        num_ref[...] = jnp.exp2((scores - peak) * gain).astype(BF16)
        shift_ref[...] = peak * gain


def share(e, p_own, x, held, gain):
    docs, width = e.shape
    own = p_own.shape[0]
    return pl.pallas_call(
        functools.partial(share_kernel, gain),
        grid=(docs // DOC_TILE,),
        in_specs=[pl.BlockSpec((DOC_TILE, width), lambda i: (i, 0))] + [whole()] * 3,
        out_specs=[
            pl.BlockSpec((own, DOC_TILE), lambda i: (0, i)),
            pl.BlockSpec((1, DOC_TILE), lambda i: (0, i)),
            whole(),
            whole(),
        ],
        out_shape=[
            pltpu.HBM((own, docs), BF16),
            pltpu.VMEM((1, docs), F32),
            pltpu.VMEM(x.shape, F32),
            pltpu.VMEM(held.shape, held.dtype),
        ],
        input_output_aliases={3: 3},
        compiler_params=params(),
    )(e, in_vmem(p_own), in_vmem(x), in_vmem(held))


def apply_kernel(x_ref, *refs):
    nums, shifts, tables = refs[:HELD], refs[HELD : 2 * HELD], refs[2 * HELD : 3 * HELD]
    out_ref, x_out = refs[3 * HELD :]
    docs = nums[0].shape[1]

    @pl.when(pl.program_id(0) == 0)
    def _():
        x_out[...] = x_ref[...]

    part = jnp.zeros(out_ref.shape, F32)
    for k in range(HELD):
        weight = jnp.exp2(shifts[k][...] + x_ref[:, k * docs : (k + 1) * docs])
        scaled = (nums[k][...].astype(F32) * weight).astype(BF16)
        part += jnp.dot(scaled, tables[k][...], preferred_element_type=F32)
    out_ref[...] = part


def apply(nums, shifts, tables, x):
    own, docs = nums[0].shape
    width = tables[0].shape[1]
    rows = min(UPDATE_ROWS, own)
    return pl.pallas_call(
        apply_kernel,
        grid=(own // rows,),
        in_specs=[whole()]
        + [pl.BlockSpec((rows, docs), lambda i: (i, 0))] * HELD
        + [whole()] * HELD
        + [pl.BlockSpec((docs, width), lambda i: (0, 0))] * HELD,
        out_specs=[pl.BlockSpec((rows, width), lambda i: (i, 0)), whole()],
        out_shape=[pltpu.HBM((own, width), F32), pltpu.VMEM(x.shape, F32)],
        compiler_params=params(),
    )(in_vmem(x), *nums, *[in_vmem(shift) for shift in shifts], *tables)


def update_kernel(gain, place_ref, e_ref, v_ref, p_ref, cs_ref, before_ref, *refs):
    out_ref, scores, acc, before, arrived = refs
    step = pl.program_id(0)
    own = p_ref.shape[0]
    size = scores.shape[1]
    places = [slice(d, d + size) for d in range(0, own, size)]
    copy = pltpu.make_async_copy(before_ref, before, arrived)

    def add(place, part):
        acc[place, :] += jnp.dot(part.astype(BF16), e_ref[...], preferred_element_type=F32)

    @pl.when(step == 0)
    def _():
        acc[...] = jnp.zeros_like(acc)
        copy.start()

    def score(j):
        scores[j % 2] = transposed_dot(p_ref[places[j], :], e_ref[...])

    score(0)
    for j in range(len(places)):
        if j + 1 < len(places):
            score(j + 1)
        add(places[j], jnp.exp2(scores[j % 2] * gain + v_ref[...]))

    @pl.when(step == pl.num_programs(0) - 1)
    def _():
        copy.wait()
        lane = lax.broadcasted_iota(jnp.int32, cs_ref.shape, 1)
        chunks = own // CHUNK
        for k in range(chunks):
            here = jnp.where(lane == place_ref[0] * chunks + k, cs_ref[...], 0.0)
            place = slice(k * CHUNK, (k + 1) * CHUNK)
            summed = (acc[place, :] + before[place, :]) * jnp.sum(here, axis=1, keepdims=True)
            square = jnp.mean(summed * summed, axis=1, keepdims=True)
            out_ref[place, :] = (summed * lax.rsqrt(square + 1e-06)).astype(BF16)


def update(place, docs, e_all, v, p_own, cs, before, gain):
    own, width = p_own.shape
    size = min(UPDATE_ROWS, own)
    ranks = e_all.shape[0] // docs

    return pl.pallas_call(
        functools.partial(update_kernel, gain),
        grid_spec=pltpu.PrefetchScalarGridSpec(
            num_scalar_prefetch=1,
            grid=(ranks - HELD,),
            in_specs=[
                pl.BlockSpec(
                    (docs, width), lambda i, place: (jnp.bitwise_xor(place[0], i + HELD), 0)
                ),
                pl.BlockSpec((1, docs), lambda i, place: (0, i + HELD)),
            ]
            + [whole()] * 2
            + [pl.BlockSpec(memory_space=pl.ANY)],
            out_specs=pl.BlockSpec((own, width), lambda i, place: (0, 0)),
            scratch_shapes=[
                pltpu.VMEM((2, size, docs), F32),
                pltpu.VMEM((own, width), F32),
                pltpu.VMEM((own, width), F32),
                pltpu.SemaphoreType.DMA,
            ],
        ),
        out_shape=jax.ShapeDtypeStruct((own, width), BF16),
        compiler_params=params(),
    )(
        place,
        in_hbm(e_all),
        v,
        in_vmem(p_own),
        in_vmem(cs),
        in_hbm(before),
    )


def swap(x, axis, bit):
    size = lax.axis_size(axis)
    return lax.ppermute(x, axis, [(i, i ^ bit) for i in range(size)])


def bits(axis):
    bit = 1
    while bit < lax.axis_size(axis):
        yield bit
        bit *= 2


def reduce_over(x, axis, combine):
    for bit in bits(axis):
        x = combine(x, swap(x, axis, bit))
    return x


def gather_over(x, axis, jobs={}):
    for bit in bits(axis):
        other = swap(x, axis, bit)
        for job in jobs.get(bit, ()):
            x = job(x)
        x = jnp.concatenate([x, other], axis=1)
    return x


def sum_over_docs(mine, other, jobs={}):
    mine = mine + swap(other, "docs", 1)
    for bit in list(bits("docs"))[1:]:
        arrived = swap(mine, "docs", bit)
        for job in jobs.get(bit, ()):
            mine = job(mine)
        mine = mine + arrived
    return mine, swap(mine, "docs", 1)


def log_add(a, b):
    top = jnp.maximum(a, b)
    return top + jnp.log2(jnp.exp2(a - top) + jnp.exp2(b - top))


def on_device(embeddings, prototypes):
    docs, width = embeddings.shape
    protos = prototypes.shape[0]
    doc_ranks = lax.axis_size("docs")
    total_docs = docs * doc_ranks
    total_protos = protos * lax.axis_size("protos")
    own = protos // doc_ranks
    gain = 4.0 / math.sqrt(width) / math.log(2.0)

    place = lax.axis_index("docs").astype(jnp.int32)

    e_all = lax.all_gather(embeddings, "docs", tiled=True)
    partner = swap(embeddings, "docs", 1)
    state = {}
    nums, shifts = [None] * HELD, [None] * HELD

    def share_job(k):
        def job(x):
            e = in_hbm(partner)
            nums[k], shifts[k], x, state["num"] = share(e, state["own"], x, state["num"], gain)
            return x

        return job

    doc_bits = list(bits("docs"))
    early = {doc_bits[1]: [share_job(1)]}

    num, shift, lse, own_table = stats(
        place.reshape(1), own, in_hbm(embeddings), in_hbm(prototypes), gain
    )
    state["own"], state["num"] = own_table, num
    lse = reduce_over(lse, "protos", log_add)
    w = jnp.exp2(shift - lse)
    weight = w
    for sweep_index in range(SWEEPS):
        beside = early if sweep_index == 0 else {}
        state["num"], *parts = columns(in_vmem(state["num"]), weight, place.reshape(1))
        mine, other = sum_over_docs(*parts, beside)
        state["num"], row_local, cs, *taken = row_sums(
            in_vmem(state["num"]),
            w,
            mine,
            other,
            place.reshape(1),
            float(total_protos),
            0 if sweep_index else own,
        )
        if taken:
            nums[0], shifts[0] = taken[0], shift
        row_sum = reduce_over(row_local, "protos", jnp.add)
        r = 1.0 / (total_docs * row_sum)
        weight = w * r

    def apply_job(x):
        tables = [in_hbm(embeddings), in_hbm(partner)]
        state["part"], x = apply([in_hbm(num) for num in nums], shifts, tables, x)
        return x

    v = gather_over(jnp.log2(r * total_docs) - lse, "docs", {doc_bits[2]: [apply_job]})
    new_prototypes = update(
        place.reshape(1), docs, e_all, v, state["own"], cs, state["part"], gain
    )
    column_potential = jnp.log(total_docs * cs.T.reshape(-1)[:protos])
    row_potential = jnp.log(lax.optimization_barrier(r)).reshape(-1)
    return (new_prototypes, column_potential, row_potential)


def solution(mesh):
    placed = (P("docs", None), P("protos", None))
    return jax.shard_map(
        on_device,
        mesh=mesh,
        in_specs=placed,
        out_specs=(P(("protos", "docs"), None), P("protos"), P("docs")),
        check_vma=False,
    )
```
